32 devices in a mesh: groups: 2 (over y), long: 4 (over z), short: 4 (over x, core).
Axes of the slice: x: 2, y: 2, z: 4, core: 2. Of those that a mesh axis runs over, the one named last changes fastest.
Arguments:
- hidden_in: bfloat16 [128, 8192], P('groups', ('short', 'long')), parts along dimension 0, may hold values from -6 to 6
- mixer_gain: bfloat16 [8192], P(('short', 'long')), may hold values from 0.099609375 to 1.8984375
- mlp_gain: bfloat16 [8192], P(('short', 'long')), may hold values from 0.099609375 to 1.8984375
- gate_in_weight: bfloat16 [8192, 2, 8192], P('short', None, 'long'), may hold values from -0.0625 to 0.0625
- group_weight: bfloat16 [8192, 1024], P('short', 'long'), may hold values from -0.0625 to 0.0625
- step_weight: bfloat16 [8192, 128], P('short', 'long'), may hold values from -0.0625 to 0.0625
- step_bias: float32 [128], P(('long', 'short')), may hold values from -5 to 0
- decay_log: float32 [128], P(('long', 'short')), may hold values from 0 to 2.77
- skip_scale: float32 [128], P(('long', 'short')), may hold values from 0.5 to 2
- conv_weight: float32 [4, 8192], P(None, ('long', 'short')), may hold values from -3 to 3
- group_conv_weight: float32 [4, 1024], P(None, 'long'), may hold values from -3 to 3
- conv_state: float32 [128, 3, 8192], P('groups', None, ('long', 'short')), parts along dimension 0, may hold values from -6 to 6
- group_conv_state: float32 [128, 3, 1024], P('groups', None, 'long'), parts along dimension 0, may hold values from -6 to 6
- ssm_state: float32 [128, 128, 64, 128], P('groups', ('long', 'short')), parts along dimension 0, may hold values from -6 to 6
- norm_gain: float32 [8192], P(('long', 'short')), may hold values from 0.1 to 1.9
- out_weight: bfloat16 [8192, 8192], P('long', 'short'), may hold values from -0.09375 to 0.09375
- up_weight: bfloat16 [8192, 16384], P('short', 'long'), may hold values from -0.0625 to 0.0625
- down_weight: bfloat16 [16384, 8192], P('long', 'short'), may hold values from -0.0625 to 0.0625
Outputs:
- hidden_out: bfloat16 [128, 8192], P('groups', ('short', 'long')), parts along dimension 0
- new_ssm_state: float32 [128, 128, 64, 128], P('groups', ('long', 'short')), parts along dimension 0
- new_conv_state: float32 [128, 3, 8192], P('groups', None, ('long', 'short')), parts along dimension 0
- new_group_conv_state: float32 [128, 3, 1024], P('groups', None, 'long'), parts along dimension 0
The draws below stay inside these ranges and needn't reach their ends.
There are 2 independent parts, one for each index of `groups`. The reference program is written for one: setup_inputs(seed, part) draws one part's arguments, and reference() takes and returns one part's arrays. A program takes and returns all parts, laid end to end along the dimension named above; an argument that names none is the same for every part. Nothing has to cross between parts.
All inputs are finite; a program needn't handle non-finite values.
Results may differ from the reference program's by a relative error of at most 0.0075.
Values may be sent and summed in bfloat16 or wider, within the bound.
No kernel may reach another device: no remote copies, remote signals or barrier semaphores. Data moves between devices by JAX's collectives and lax.ppermute only.
A program may use at most 192 MiB of HBM per device.

```python
import jax
import jax.numpy as jnp
from jax import lax

WIDTH = 8192
HEADS = 128
HEAD_DIM = 64
STATE = 128
GROUPS = 4
FFN = 16384
KERNEL = 4
ROWS = 64
INNER = 8192
BCW = 1024


def spiked(result, stream_key, source, target, parts, factor):
    def block_of(position):
        return (jnp.arange(result.shape[position]) // (result.shape[position] // parts)).reshape((-1,) + (1,) * (result.ndim - 1 - position))

    first = jax.random.permutation(stream_key, parts)[block_of(target)]
    far = (block_of(target) + parts // 2) % parts
    return jnp.where((block_of(source) == first) | (block_of(source) == far), factor * result, result)


def shard_levels(stream_key, shape, pieces, low, top_value):
    loudness = 1.0
    for position, parts in pieces:
        steps = jax.random.uniform(jax.random.fold_in(jax.random.fold_in(stream_key, 6), position), (parts,), jnp.float32, low / len(pieces), top_value / len(pieces))
        loudness = loudness * jnp.repeat(jnp.exp(steps), shape[position] // parts).reshape((-1,) + (1,) * (len(shape) - 1 - position))
    return loudness


def normal_values(own_key, extent, spread, most, cuts=(), dtype=jnp.bfloat16):
    level = shard_levels(own_key, extent, cuts, -0.22, 0.18) if cuts else 1.0
    drawn = jax.random.normal(own_key, extent, jnp.float32) * spread * level
    return jnp.minimum(jnp.maximum(drawn, -most), most).astype(dtype)


def heavy_noise(key, dims, width, reach, split, heavy, dtype=jnp.bfloat16):
    drawn = width * jax.random.normal(key, dims, jnp.float32)
    if split:
        drawn = drawn * shard_levels(key, dims, split, -0.22, 0.18)
    return jnp.clip(spiked(drawn, jax.random.fold_in(key, 3), *heavy), -reach, reach).astype(dtype)


def setup_inputs(seed: int = 0, part: int = 0) -> dict:
    streams_of = jax.random.split(jax.random.key(seed), 19)
    part_keys = jax.random.split(jax.random.fold_in(streams_of[18], part), 19)
    hidden_in = normal_values(part_keys[0], (ROWS, WIDTH), 1.0, 6.0, ((1, 16),))
    mixer_gain = jnp.clip(1.0 + 0.18 * jax.random.normal(streams_of[1], (WIDTH,), jnp.float32), 0.099609375, 1.8984375).astype(jnp.bfloat16)
    mlp_gain = jnp.clip(1.0 + 0.18 * jax.random.normal(streams_of[2], (WIDTH,), jnp.float32), 0.099609375, 1.8984375).astype(jnp.bfloat16)
    gate_in_weight = normal_values(streams_of[3], (WIDTH, 2, INNER), WIDTH ** -0.5, 0.0625, ((0, 4), (2, 4)))
    group_weight = normal_values(streams_of[4], (WIDTH, BCW), WIDTH ** -0.5, 0.0625, ((0, 4), (1, 4)))
    step_weight = normal_values(streams_of[5], (WIDTH, HEADS), WIDTH ** -0.5, 0.0625, ((0, 4), (1, 4)))
    step_bias = jnp.clip(-5.0 + 5.0 * jax.random.uniform(streams_of[6], (HEADS,), jnp.float32) ** shard_levels(streams_of[6], (HEADS,), ((0, 16),), -0.2, 0.2), -5.0, 0.0)
    decay_log = jnp.clip(2.77 * jax.random.uniform(streams_of[7], (HEADS,), jnp.float32) ** shard_levels(streams_of[7], (HEADS,), ((0, 16),), -0.2, 0.2), 0.0, 2.77)
    skip_scale = jnp.clip(0.5 + 1.5 * jax.random.uniform(streams_of[8], (HEADS,), jnp.float32) ** shard_levels(streams_of[8], (HEADS,), ((0, 16),), -0.2, 0.2), 0.5, 2.0)
    conv_weight = normal_values(streams_of[9], (KERNEL, INNER), 0.5, 3.0, ((1, 16),), jnp.float32)
    group_conv_weight = normal_values(streams_of[10], (KERNEL, BCW), 0.5, 3.0, ((1, 4),), jnp.float32)
    conv_state = normal_values(part_keys[11], (ROWS, KERNEL - 1, INNER), 1.0, 6.0, ((2, 16),), jnp.float32)
    group_conv_state = normal_values(part_keys[12], (ROWS, KERNEL - 1, BCW), 1.0, 6.0, ((2, 4),), jnp.float32)
    ssm_state = normal_values(part_keys[13], (ROWS, HEADS, HEAD_DIM, STATE), 1.0, 6.0, ((1, 16),), jnp.float32)
    norm_gain = jnp.clip(1.0 + 0.18 * jax.random.normal(streams_of[14], (INNER,), jnp.float32), 0.1, 1.9)
    out_weight = heavy_noise(streams_of[15], (INNER, WIDTH), INNER ** -0.5, 0.09375, ((0, 4), (1, 4)), (0, 1, 4, 2.0))
    up_weight = normal_values(streams_of[16], (WIDTH, FFN), WIDTH ** -0.5, 0.0625, ((0, 4), (1, 4)))
    down_weight = heavy_noise(streams_of[17], (FFN, WIDTH), FFN ** -0.5, 0.0625, ((0, 4), (1, 4)), (0, 1, 4, 2.0))
    return dict(hidden_in=hidden_in, mixer_gain=mixer_gain, mlp_gain=mlp_gain, gate_in_weight=gate_in_weight, group_weight=group_weight, step_weight=step_weight, step_bias=step_bias, decay_log=decay_log, skip_scale=skip_scale, conv_weight=conv_weight, group_conv_weight=group_conv_weight, conv_state=conv_state, group_conv_state=group_conv_state, ssm_state=ssm_state, norm_gain=norm_gain, out_weight=out_weight, up_weight=up_weight, down_weight=down_weight)


epsilon = 1e-05

def reference(hidden_in, mixer_gain, mlp_gain, gate_in_weight, group_weight, step_weight, step_bias, decay_log, skip_scale, conv_weight, group_conv_weight, conv_state, group_conv_state, ssm_state, norm_gain, out_weight, up_weight, down_weight):
    features = hidden_in.astype(jnp.float32)
    scaled = (features * mixer_gain.astype(jnp.float32)).astype(jnp.bfloat16)
    inverse = lax.rsqrt(lax.optimization_barrier(jnp.mean(features * features, axis=1)) + epsilon)[:, None]
    gate_in = jnp.dot(scaled, gate_in_weight.reshape(WIDTH, 2 * INNER), preferred_element_type=jnp.float32) * inverse
    gate_in = gate_in.reshape(ROWS, 2, INNER)
    group_raw = jnp.dot(scaled, group_weight, preferred_element_type=jnp.float32) * inverse
    step_raw = jnp.dot(scaled, step_weight, preferred_element_type=jnp.float32) * inverse
    window = jnp.concatenate([conv_state, gate_in[:, 1][:, None, :]], axis=1)
    mixer_input = jax.nn.silu(lax.optimization_barrier(jnp.sum(window * conv_weight[None], axis=1)))
    group_window = jnp.concatenate([group_conv_state, group_raw[:, None, :]], axis=1)
    group_act = jax.nn.silu(lax.optimization_barrier(jnp.sum(group_window * group_conv_weight[None], axis=1)))
    per_group = HEADS // GROUPS
    state_in = jnp.repeat(group_act[:, :GROUPS * STATE].reshape(ROWS, GROUPS, STATE), per_group, axis=1)
    state_out = jnp.repeat(group_act[:, GROUPS * STATE:].reshape(ROWS, GROUPS, STATE), per_group, axis=1)
    step = jax.nn.softplus(step_raw + step_bias[None])
    decay = jnp.exp(-jnp.exp(decay_log)[None] * step)
    head_input = mixer_input.reshape(ROWS, HEADS, HEAD_DIM)
    new_state = decay[:, :, None, None] * ssm_state + (step[:, :, None] * head_input)[:, :, :, None] * state_in[:, :, None, :]
    readout = jnp.einsum('rhpn,rhn->rhp', new_state, state_out, precision=lax.Precision.HIGHEST)
    readout = readout + skip_scale[None, :, None] * head_input
    readout = readout.reshape(ROWS, INNER) * jax.nn.silu(gate_in[:, 0])
    grouped = readout.reshape(ROWS, GROUPS, INNER // GROUPS)
    group_mean = lax.optimization_barrier(jnp.mean(grouped * grouped, axis=2))
    normed = (grouped * lax.rsqrt(group_mean + epsilon)[:, :, None]).reshape(ROWS, INNER) * norm_gain[None]
    normed = normed.astype(jnp.bfloat16)
    mixed = jnp.dot(normed, out_weight, preferred_element_type=jnp.float32)
    middle = (features + mixed).astype(jnp.bfloat16)
    middle_f = middle.astype(jnp.float32)
    scaled_mid = (middle_f * mlp_gain.astype(jnp.float32)).astype(jnp.bfloat16)
    inverse_mid = lax.rsqrt(lax.optimization_barrier(jnp.mean(middle_f * middle_f, axis=1)) + epsilon)[:, None]
    upward = jnp.dot(scaled_mid, up_weight, preferred_element_type=jnp.float32) * inverse_mid
    active = jnp.square(jnp.maximum(upward, 0.0)).astype(jnp.bfloat16)
    downward = jnp.dot(active, down_weight, preferred_element_type=jnp.float32)
    hidden_out = (middle_f + downward).astype(jnp.bfloat16)
    return (hidden_out, new_state, window[:, 1:], group_window[:, 1:])
```

```python
import jax
import jax.numpy as jnp
from jax import lax
from jax.sharding import PartitionSpec as P

WIDTH = 8192
HEADS = 128
HEAD_DIM = 64
STATE = 128
GROUPS = 4
INNER = 8192

f32 = jnp.float32
bf16 = jnp.bfloat16
epsilon = 1e-05


def swap(value, axis, bits):
    size = lax.axis_size(axis)
    return lax.ppermute(value, axis, [(i, i ^ bits) for i in range(size)])


def in_order(blocks, index):
    stacked = jnp.stack(blocks)
    bit = 1
    while bit < len(blocks):
        shape = stacked.shape
        paired = stacked.reshape((-1, 2, bit) + shape[1:])
        stacked = jnp.where((index & bit) != 0, paired[:, ::-1], paired).reshape(shape)
        bit *= 2
    return stacked


def gather(value, axis):
    size = lax.axis_size(axis)
    blocks = [value] + [swap(value, axis, k) for k in range(1, size)]
    return in_order(blocks, lax.axis_index(axis))


def scatter_sum(parts, axis):
    size = lax.axis_size(axis)
    index = lax.axis_index(axis)
    total = lax.dynamic_index_in_dim(parts, index, 0, False)
    sent = parts.astype(bf16)
    for k in range(size - 1, 0, -1):
        block = lax.dynamic_index_in_dim(sent, index ^ k, 0, False)
        total = total + swap(block, axis, k).astype(f32)
    return total


def chip_scatter_sum(parts, axis):
    size = lax.axis_size(axis)
    index = lax.axis_index(axis)
    parts = parts.reshape((size // 2, 2) + parts.shape[1:])
    mine = lax.dynamic_index_in_dim(parts, index & 1, 1, False)
    other = lax.dynamic_index_in_dim(parts, (index & 1) ^ 1, 1, False)
    parts = mine + swap(other.astype(bf16), axis, 1).astype(f32)
    total = lax.dynamic_index_in_dim(parts, index // 2, 0, False)
    sent = parts.astype(bf16)
    for k in range(size // 2 - 1, 0, -1):
        block = lax.dynamic_index_in_dim(sent, (index // 2) ^ k, 0, False)
        total = total + swap(block, axis, 2 * k).astype(f32)
    return total


def total_over(value, axis):
    bit = 1
    while bit < lax.axis_size(axis):
        value = value + swap(value, axis, bit)
        bit *= 2
    return value


def split_pair(value):
    high = value.astype(bf16)
    return high, (value - high.astype(f32)).astype(bf16)


def with_square(block, square):
    high, low = split_pair(square)
    rows = block.shape[0]
    lanes = lax.broadcasted_iota(jnp.int32, (rows, 128), 1)
    tail = jnp.where(lanes == 0, high[:, None], jnp.where(lanes == 1, low[:, None], 0))
    return jnp.concatenate([block, tail.astype(bf16)], axis=1)


def square_of(tail):
    return tail[..., 0].astype(f32) + tail[..., 1].astype(f32)


def local(
    hidden_in,
    mixer_gain,
    mlp_gain,
    gate_in_weight,
    group_weight,
    step_weight,
    step_bias,
    decay_log,
    skip_scale,
    conv_weight,
    group_conv_weight,
    conv_state,
    group_conv_state,
    ssm_state,
    norm_gain,
    out_weight,
    up_weight,
    down_weight,
):
    rows = hidden_in.shape[0]
    longs, shorts = lax.axis_size("long"), lax.axis_size("short")
    at_long, at_short = lax.axis_index("long"), lax.axis_index("short")
    own = hidden_in.shape[1]

    features = hidden_in.astype(f32)
    scaled_own = (features * mixer_gain.astype(f32)).astype(bf16)
    blocks = gather(with_square(scaled_own, jnp.sum(features * features, axis=1)), "long")
    scaled = jnp.transpose(blocks[:, :, :own], (1, 0, 2)).reshape(rows, longs * own)
    square = jnp.sum(square_of(blocks[:, :, own:]), axis=0)

    part_groups = jnp.dot(scaled, group_weight, preferred_element_type=f32)
    part_steps = jnp.dot(scaled, step_weight, preferred_element_type=f32)
    small = total_over(jnp.concatenate([part_groups, part_steps, square[:, None]], axis=1), "short")
    wide = part_groups.shape[1]
    inverse = lax.rsqrt(small[:, -1:] / WIDTH + epsilon)
    group_raw = small[:, :wide] * inverse
    steps_here = part_steps.shape[1] // shorts
    step_raw = lax.dynamic_slice_in_dim(small, wide + at_short * steps_here, steps_here, 1) * inverse

    part_gates = jnp.einsum("rd,dkc->krc", scaled, gate_in_weight, preferred_element_type=f32)
    mixed_width = part_gates.shape[2] // shorts
    part_gates = jnp.transpose(part_gates.reshape(2, rows, shorts, mixed_width), (2, 0, 1, 3))
    gate_in = chip_scatter_sum(part_gates, "short") * inverse

    group_window = jnp.concatenate([group_conv_state, group_raw[:, None, :]], axis=1)
    group_act = jax.nn.silu(jnp.sum(group_window * group_conv_weight[None], axis=1))
    heads_here = mixed_width // HEAD_DIM
    first_head = (at_long * shorts + at_short) * heads_here
    group_index = first_head // (HEADS // GROUPS)
    group_full = gather(group_act, "long")
    group_full = jnp.transpose(group_full, (1, 0, 2)).reshape(rows, longs * wide)
    state_in = lax.dynamic_slice_in_dim(group_full, group_index * STATE, STATE, 1)
    state_out = lax.dynamic_slice_in_dim(group_full, (GROUPS + group_index) * STATE, STATE, 1)

    step_size = jax.nn.softplus(step_raw + step_bias[None])
    decay = jnp.exp(-jnp.exp(decay_log)[None] * step_size)
    window = jnp.concatenate([conv_state, gate_in[1][:, None, :]], axis=1)
    mixer_input = jax.nn.silu(jnp.sum(window * conv_weight[None], axis=1))
    head_input = mixer_input.reshape(rows, heads_here, HEAD_DIM)
    new_state = (
        decay[:, :, None, None] * ssm_state
        + (step_size[:, :, None] * head_input)[:, :, :, None] * state_in[:, None, None, :]
    )
    readout = jnp.sum(new_state * state_out[:, None, None, :], axis=-1)
    readout = readout + skip_scale[None, :, None] * head_input
    readout = readout.reshape(rows, heads_here * HEAD_DIM) * jax.nn.silu(gate_in[0])

    local_square = jnp.sum(readout * readout, axis=1)
    unscaled = (readout * norm_gain[None]).astype(bf16)
    blocks = gather(with_square(unscaled, local_square), "short")
    wide_own = unscaled.shape[1]
    normed = jnp.transpose(blocks[:, :, :wide_own], (1, 0, 2)).reshape(rows, shorts * wide_own)
    group_square = jnp.sum(square_of(blocks[:, :, wide_own:]), axis=0)
    if longs > GROUPS:
        mine = jnp.arange(GROUPS) == group_index
        totals = lax.psum(jnp.where(mine[None], group_square[:, None], 0.0), "long")
        group_square = jnp.sum(jnp.where(mine[None], totals, 0.0), axis=1)
    group_scale = lax.rsqrt(group_square / (INNER // GROUPS) + epsilon)
    part_mixed = jnp.dot(normed, out_weight, preferred_element_type=f32) * group_scale[:, None]
    part_mixed = jnp.transpose(part_mixed.reshape(rows, longs, own), (1, 0, 2))
    middle_own = (features + scatter_sum(part_mixed, "long")).astype(bf16)
    middle = middle_own.astype(f32)

    scaled_own = (middle * mlp_gain.astype(f32)).astype(bf16)
    blocks = gather(with_square(scaled_own, jnp.sum(middle * middle, axis=1)), "long")
    scaled_mid = jnp.transpose(blocks[:, :, :own], (1, 0, 2)).reshape(rows, longs * own)
    middle_square = jnp.sum(square_of(blocks[:, :, own:]), axis=0)

    part_up = jnp.dot(scaled_mid, up_weight, preferred_element_type=f32)
    half = part_up.shape[1] // 2
    core = at_short & 1
    mine = lax.dynamic_slice_in_dim(part_up, core * half, half, 1)
    other = lax.dynamic_slice_in_dim(part_up, (core ^ 1) * half, half, 1).astype(bf16)
    arrived = swap(with_square(other, middle_square), "short", 1)
    upward = mine + arrived[:, :half].astype(f32)
    middle_square = middle_square + square_of(arrived[:, half:])
    sent = with_square(upward.astype(bf16), middle_square)
    for k in range(1, shorts // 2):
        arrived = swap(sent, "short", 2 * k)
        upward = upward + arrived[:, :half].astype(f32)
        middle_square = middle_square + square_of(arrived[:, half:])
    inverse_mid = lax.rsqrt(middle_square / WIDTH + epsilon)[:, None]
    active_half = jnp.square(jnp.maximum(upward * inverse_mid, 0.0)).astype(bf16)
    pair = in_order([active_half, swap(active_half, "short", 1)], core)
    active = jnp.concatenate([pair[0], pair[1]], axis=1)

    part_down = jnp.dot(active, down_weight, preferred_element_type=f32)
    part_down = jnp.transpose(part_down.reshape(rows, longs, own), (1, 0, 2))
    hidden_out = (middle + scatter_sum(part_down, "long")).astype(bf16)
    return (hidden_out, new_state, window[:, 1:], group_window[:, 1:])


def solution(mesh):
    placed = (
        P("groups", ("short", "long")),
        P(("short", "long")),
        P(("short", "long")),
        P("short", None, "long"),
        P("short", "long"),
        P("short", "long"),
        P(("long", "short")),
        P(("long", "short")),
        P(("long", "short")),
        P(None, ("long", "short")),
        P(None, "long"),
        P("groups", None, ("long", "short")),
        P("groups", None, "long"),
        P("groups", ("long", "short"), None, None),
        P(("long", "short")),
        P("long", "short"),
        P("short", "long"),
        P("long", "short"),
    )
    return jax.shard_map(
        local,
        mesh=mesh,
        in_specs=placed,
        out_specs=(
            P("groups", ("short", "long")),
            P("groups", ("long", "short"), None, None),
            P("groups", None, ("long", "short")),
            P("groups", None, "long"),
        ),
        check_vma=False,
    )
```

```python
import functools

import jax
import jax.numpy as jnp
from jax import lax
from jax.experimental import pallas as pl
from jax.experimental.pallas import tpu as pltpu
from jax.sharding import PartitionSpec as P

WIDTH = 8192
HEADS = 128
HEAD_DIM = 64
STATE = 128
GROUPS = 4
INNER = 8192

f32 = jnp.float32
bf16 = jnp.bfloat16
epsilon = 1e-05


def swap(value, axis, bits):
    size = lax.axis_size(axis)
    return lax.ppermute(value, axis, [(i, i ^ bits) for i in range(size)])


def in_order(blocks, index):
    stacked = jnp.stack(blocks)
    bit = 1
    while bit < len(blocks):
        shape = stacked.shape
        paired = stacked.reshape((-1, 2, bit) + shape[1:])
        stacked = jnp.where((index & bit) != 0, paired[:, ::-1], paired).reshape(shape)
        bit *= 2
    return stacked


def gather(value, axis):
    size = lax.axis_size(axis)
    blocks = [value] + [swap(value, axis, k) for k in range(1, size)]
    return in_order(blocks, lax.axis_index(axis))


def scatter_sum(parts, axis):
    size = lax.axis_size(axis)
    index = lax.axis_index(axis)
    total = lax.dynamic_index_in_dim(parts, index, 0, False)
    sent = parts.astype(bf16)
    for k in range(size - 1, 0, -1):
        block = lax.dynamic_index_in_dim(sent, index ^ k, 0, False)
        total = total + swap(block, axis, k).astype(f32)
    return total


def chip_scatter_sum(parts, axis):
    size = lax.axis_size(axis)
    index = lax.axis_index(axis)
    parts = parts.reshape((size // 2, 2) + parts.shape[1:])
    mine = lax.dynamic_index_in_dim(parts, index & 1, 1, False)
    other = lax.dynamic_index_in_dim(parts, (index & 1) ^ 1, 1, False)
    parts = mine + swap(other.astype(bf16), axis, 1).astype(f32)
    total = lax.dynamic_index_in_dim(parts, index // 2, 0, False)
    sent = parts.astype(bf16)
    for k in range(size // 2 - 1, 0, -1):
        block = lax.dynamic_index_in_dim(sent, (index // 2) ^ k, 0, False)
        total = total + swap(block, axis, 2 * k).astype(f32)
    return total


def total_over(value, axis):
    bit = 1
    while bit < lax.axis_size(axis):
        value = value + swap(value, axis, bit)
        bit *= 2
    return value


def split_pair(value):
    high = value.astype(bf16)
    return high, (value - high.astype(f32)).astype(bf16)


def with_square(block, square):
    high, low = split_pair(square)
    rows = block.shape[0]
    lanes = lax.broadcasted_iota(jnp.int32, (rows, 128), 1)
    tail = jnp.where(lanes == 0, high[:, None], jnp.where(lanes == 1, low[:, None], 0))
    return jnp.concatenate([block, tail.astype(bf16)], axis=1)


def square_of(tail):
    return tail[..., 0].astype(f32) + tail[..., 1].astype(f32)


def local(
    hidden_in,
    mixer_gain,
    mlp_gain,
    gate_in_weight,
    group_weight,
    step_weight,
    step_bias,
    decay_log,
    skip_scale,
    conv_weight,
    group_conv_weight,
    conv_state,
    group_conv_state,
    ssm_state,
    norm_gain,
    out_weight,
    up_weight,
    down_weight,
):
    rows = hidden_in.shape[0]
    longs, shorts = lax.axis_size("long"), lax.axis_size("short")
    at_long, at_short = lax.axis_index("long"), lax.axis_index("short")
    own = hidden_in.shape[1]

    features = hidden_in.astype(f32)
    scaled_own = (features * mixer_gain.astype(f32)).astype(bf16)
    blocks = gather(with_square(scaled_own, jnp.sum(features * features, axis=1)), "long")
    scaled = jnp.transpose(blocks[:, :, :own], (1, 0, 2)).reshape(rows, longs * own)
    square = jnp.sum(square_of(blocks[:, :, own:]), axis=0)

    part_groups = jnp.dot(scaled, group_weight, preferred_element_type=f32)
    part_steps = jnp.dot(scaled, step_weight, preferred_element_type=f32)
    small = total_over(jnp.concatenate([part_groups, part_steps, square[:, None]], axis=1), "short")
    wide = part_groups.shape[1]
    inverse = lax.rsqrt(small[:, -1:] / WIDTH + epsilon)
    group_raw = small[:, :wide] * inverse
    steps_here = part_steps.shape[1] // shorts
    step_raw = lax.dynamic_slice_in_dim(small, wide + at_short * steps_here, steps_here, 1) * inverse

    part_gates = jnp.einsum("rd,dkc->krc", scaled, gate_in_weight, preferred_element_type=f32)
    mixed_width = part_gates.shape[2] // shorts
    part_gates = jnp.transpose(part_gates.reshape(2, rows, shorts, mixed_width), (2, 0, 1, 3))
    gate_in = chip_scatter_sum(part_gates, "short") * inverse

    group_window = jnp.concatenate([group_conv_state, group_raw[:, None, :]], axis=1)
    group_act = jax.nn.silu(jnp.sum(group_window * group_conv_weight[None], axis=1))
    heads_here = mixed_width // HEAD_DIM
    first_head = (at_long * shorts + at_short) * heads_here
    group_index = first_head // (HEADS // GROUPS)
    group_full = gather(group_act, "long")
    group_full = jnp.transpose(group_full, (1, 0, 2)).reshape(rows, longs * wide)
    state_in = lax.dynamic_slice_in_dim(group_full, group_index * STATE, STATE, 1)
    state_out = lax.dynamic_slice_in_dim(group_full, (GROUPS + group_index) * STATE, STATE, 1)

    step_size = jax.nn.softplus(step_raw + step_bias[None])
    decay = jnp.exp(-jnp.exp(decay_log)[None] * step_size)
    window = jnp.concatenate([conv_state, gate_in[1][:, None, :]], axis=1)
    mixer_input = jax.nn.silu(jnp.sum(window * conv_weight[None], axis=1))
    head_input = mixer_input.reshape(rows, heads_here, HEAD_DIM)
    new_state = (
        decay[:, :, None, None] * ssm_state
        + (step_size[:, :, None] * head_input)[:, :, :, None] * state_in[:, None, None, :]
    )
    readout = jnp.sum(new_state * state_out[:, None, None, :], axis=-1)
    readout = readout + skip_scale[None, :, None] * head_input
    readout = readout.reshape(rows, heads_here * HEAD_DIM) * jax.nn.silu(gate_in[0])

    local_square = jnp.sum(readout * readout, axis=1)
    unscaled = (readout * norm_gain[None]).astype(bf16)
    blocks = gather(with_square(unscaled, local_square), "short")
    wide_own = unscaled.shape[1]
    normed = jnp.transpose(blocks[:, :, :wide_own], (1, 0, 2)).reshape(rows, shorts * wide_own)
    group_square = jnp.sum(square_of(blocks[:, :, wide_own:]), axis=0)
    if longs > GROUPS:
        mine = jnp.arange(GROUPS) == group_index
        totals = lax.psum(jnp.where(mine[None], group_square[:, None], 0.0), "long")
        group_square = jnp.sum(jnp.where(mine[None], totals, 0.0), axis=1)
    group_scale = lax.rsqrt(group_square / (INNER // GROUPS) + epsilon)
    part_mixed = jnp.dot(normed, out_weight, preferred_element_type=f32) * group_scale[:, None]
    part_mixed = jnp.transpose(part_mixed.reshape(rows, longs, own), (1, 0, 2))
    middle_own = (features + scatter_sum(part_mixed, "long")).astype(bf16)
    middle = middle_own.astype(f32)

    scaled_own = (middle * mlp_gain.astype(f32)).astype(bf16)
    blocks = gather(with_square(scaled_own, jnp.sum(middle * middle, axis=1)), "long")
    scaled_mid = jnp.transpose(blocks[:, :, :own], (1, 0, 2)).reshape(rows, longs * own)
    middle_square = jnp.sum(square_of(blocks[:, :, own:]), axis=0)

    part_up = jnp.dot(scaled_mid, up_weight, preferred_element_type=f32)
    half = part_up.shape[1] // 2
    core = at_short & 1
    mine = lax.dynamic_slice_in_dim(part_up, core * half, half, 1)
    other = lax.dynamic_slice_in_dim(part_up, (core ^ 1) * half, half, 1).astype(bf16)
    arrived = swap(with_square(other, middle_square), "short", 1)
    upward = mine + arrived[:, :half].astype(f32)
    middle_square = middle_square + square_of(arrived[:, half:])
    sent = with_square(upward.astype(bf16), middle_square)
    for k in range(1, shorts // 2):
        arrived = swap(sent, "short", 2 * k)
        upward = upward + arrived[:, :half].astype(f32)
        middle_square = middle_square + square_of(arrived[:, half:])
    inverse_mid = lax.rsqrt(middle_square / WIDTH + epsilon)[:, None]
    active_half = jnp.square(jnp.maximum(upward * inverse_mid, 0.0)).astype(bf16)
    pair = in_order([active_half, swap(active_half, "short", 1)], core)
    active = jnp.concatenate([pair[0], pair[1]], axis=1)

    part_down = jnp.dot(active, down_weight, preferred_element_type=f32)
    part_down = jnp.transpose(part_down.reshape(rows, longs, own), (1, 0, 2))
    hidden_out = (middle + scatter_sum(part_down, "long")).astype(bf16)
    return (hidden_out, new_state, window[:, 1:], group_window[:, 1:])


IN_VMEM = pl.BlockSpec(memory_space=pltpu.VMEM)
IN_PLACE = pl.BlockSpec(memory_space=pl.ANY)
IN_SMEM = pl.BlockSpec(memory_space=pltpu.SMEM)
MIB = 1 << 20


def cost_of(reads, flops):
    return pl.CostEstimate(flops=flops, bytes_accessed=reads, transcendentals=0)


def call(body, name, places, arrays, outs, flops, weight=None, scratch=(), room=8 * MIB):
    given = [*arrays] if weight is None else [*arrays, weight]
    reads = sum(a.size * a.dtype.itemsize for a in given)
    return pl.pallas_call(
        body,
        in_specs=[IN_SMEM] + [IN_VMEM] * len(arrays) + [IN_PLACE] * (weight is not None),
        out_specs=[IN_VMEM] * len(outs),
        out_shape=[jax.ShapeDtypeStruct(shape, dtype) for shape, dtype in outs],
        scratch_shapes=list(scratch),
        compiler_params=pltpu.CompilerParams(vmem_limit_bytes=room),
        cost_estimate=cost_of(reads, flops),
        name=name,
    )(jnp.stack(places).astype(jnp.int32), *given)


def started(copies):
    copies = [pltpu.make_async_copy(*copy) for copy in copies]
    for copy in copies:
        copy.start()
    return copies


def fetch_body(pieces, source, target, semaphores):
    step = source.shape[0] // pieces
    copies = [
        pltpu.make_async_copy(source.at[pl.ds(i * step, step)], target.at[pl.ds(i * step, step)], semaphores.at[i])
        for i in range(pieces)
    ]
    for copy in copies:
        copy.start()
    for copy in copies:
        copy.wait()


def fetched(weight, after, name, pieces=8):
    weight, _ = lax.optimization_barrier((weight, after))
    return pl.pallas_call(
        functools.partial(fetch_body, pieces),
        in_specs=[pl.BlockSpec(memory_space=pl.ANY)],
        out_specs=IN_VMEM,
        out_shape=jax.ShapeDtypeStruct(weight.shape, weight.dtype),
        scratch_shapes=[pltpu.SemaphoreType.DMA((pieces,))],
        compiler_params=pltpu.CompilerParams(vmem_limit_bytes=(34 if weight.size > 6 * MIB else 40) * MIB),
        cost_estimate=cost_of(2 * weight.size * weight.dtype.itemsize, 0),
        name=name,
    )(weight)


def two_columns(square):
    high, low = split_pair(square)
    lanes = lax.broadcasted_iota(jnp.int32, (square.shape[0], 128), 1)
    return jnp.where(lanes == 0, high.astype(f32), jnp.where(lanes == 1, low.astype(f32), 0.0)).astype(bf16)


def from_two(tail):
    return jnp.sum(tail[:, :2].astype(f32), axis=1, keepdims=True)


def spread_body(own, wide, heads, place, *refs):
    count = len(refs) - 4
    blocks, group_w, step_w, small, spread = refs[:count], refs[-4], refs[-3], refs[-2], refs[-1]
    rows = small.shape[0]
    index = place[0]
    groups = jnp.zeros((rows, wide), f32)
    steps = jnp.zeros((rows, heads), f32)
    square = jnp.zeros((rows, 1), f32)
    piece = 256
    unit = lax.broadcasted_iota(jnp.int32, (piece, 2 * piece), 0) * 2
    target = lax.broadcasted_iota(jnp.int32, (piece, 2 * piece), 1)
    for k in range(count):
        block = blocks[k][:, :own]
        start = pl.multiple_of((index ^ k) * own, own)
        groups += jnp.dot(block, group_w[pl.ds(start, own), :], preferred_element_type=f32)
        steps += lax.dot_general(
            block, step_w[:, pl.ds(start, own)], (((1,), (1,)), ((), ())), preferred_element_type=f32
        )
        square += from_two(blocks[k][:, own:])
    small[:, :wide] = groups
    lanes = lax.broadcasted_iota(jnp.int32, (rows, 128), 1)
    small[:, wide:] = jnp.where(lanes == 127, square, 0.0)
    small[:, wide : wide + heads] = steps
    for which in range(2):
        ones = (unit + which == target).astype(bf16)
        for k in range(count):
            for j in range(own // piece):
                part = jnp.dot(blocks[k][:, j * piece : (j + 1) * piece], ones, preferred_element_type=f32)
                spread[k, which * rows : (which + 1) * rows, 2 * j * piece : 2 * (j + 1) * piece] = part.astype(bf16)


def gates_body(own, width, place, spread, weight, mine, other, held, total, arrived):
    index, chip, core = place[0], place[1], place[2]
    count, rows = spread.shape[0], spread.shape[1] // 2
    piece = own // 2
    copies = started(
        (
            weight.at[pl.ds(pl.multiple_of((index ^ (i // 2)) * own + (i % 2) * piece, piece), piece)],
            held.at[pl.ds(i * piece, piece)],
            arrived.at[i],
        )
        for i in range(2 * count)
    )
    for i in range(2 * count):
        copies[i].wait()
        block = spread[i // 2, :, (i % 2) * 2 * piece : (i % 2 + 1) * 2 * piece]
        for t in range(2 * mine.shape[0]):
            side, q = divmod(t, mine.shape[0])
            column = pl.multiple_of((((chip ^ q) * 2) + (core ^ (1 - side))) * width, width)
            rows_of = held[i * piece : (i + 1) * piece, :, pl.ds(column, width)].reshape(2 * piece, width)
            value = jnp.dot(block, rows_of, preferred_element_type=f32)
            if i > 0:
                value += total[t]
            if i < 2 * count - 1:
                total[t] = value
                continue
            to = mine if side else other
            to[q, 0] = value[:rows].astype(to.dtype)
            to[q, 1] = value[rows:].astype(to.dtype)


def out_body(own, width, mean_over, count, place, *refs):
    blocks, weight, outs = refs[:count], refs[count], refs[count + 1 :]
    at_short, at_long = place[0], place[1]
    square = from_two(blocks[0][:, width:])
    for k in range(1, count):
        square += from_two(blocks[k][:, width:])
    scale = lax.rsqrt(square / mean_over + epsilon)
    for q in range(len(outs) - 1, -1, -1):
        column = pl.multiple_of((at_long ^ q) * own, own)
        total = jnp.zeros(outs[q].shape, f32)
        for k in range(count):
            start = pl.multiple_of((at_short ^ k) * width, width)
            total += jnp.dot(
                blocks[k][:, :width], weight[pl.ds(start, width), pl.ds(column, own)], preferred_element_type=f32
            )
        outs[q][...] = (total * scale).astype(outs[q].dtype)


def up_body(own, place, *refs):
    count = len(refs) - 3
    blocks, weight, mine, other = refs[:count], refs[-3], refs[-2], refs[-1]
    index, core = place[0], place[1]
    half = weight.shape[1] // 2
    piece = 512
    square = from_two(blocks[0][:, own:])
    for k in range(1, count):
        square += from_two(blocks[k][:, own:])
    for side in range(2):
        for j in range(half // piece):
            column = pl.multiple_of((core ^ (1 - side)) * half + j * piece, piece)
            total = jnp.zeros((mine.shape[0], piece), f32)
            for k in range(count):
                start = pl.multiple_of((index ^ k) * own, own)
                total += jnp.dot(
                    blocks[k][:, :own], weight[pl.ds(start, own), pl.ds(column, piece)], preferred_element_type=f32
                )
            if side == 0:
                other[:, j * piece : (j + 1) * piece] = total.astype(bf16)
            else:
                mine[:, j * piece : (j + 1) * piece] = total
    other[:, half:] = two_columns(square)
    mine[:, half:] = jnp.broadcast_to(square, (square.shape[0], 128))


def down_body(own, place, first, second, weight, *outs):
    core, at_long = place[0], place[1]
    half = first.shape[1]
    for q in range(len(outs) - 1, -1, -1):
        column = pl.multiple_of((at_long ^ q) * own, own)
        total = jnp.zeros(outs[q].shape, f32)
        for k, block in enumerate((first, second)):
            start = pl.multiple_of((core ^ k) * half, half)
            total += jnp.dot(block[...], weight[pl.ds(start, half), pl.ds(column, own)], preferred_element_type=f32)
        outs[q][...] = total.astype(outs[q].dtype)


def exchanged(value, axis):
    return [value] + [swap(value, axis, k) for k in range(1, lax.axis_size(axis))]


def fast(
    hidden_in,
    mixer_gain,
    mlp_gain,
    gate_in_weight,
    group_weight,
    step_weight,
    step_bias,
    decay_log,
    skip_scale,
    conv_weight,
    group_conv_weight,
    conv_state,
    group_conv_state,
    ssm_state,
    norm_gain,
    out_weight,
    up_weight,
    down_weight,
):
    rows, own = hidden_in.shape
    longs, shorts = lax.axis_size("long"), lax.axis_size("short")
    at_long, at_short = lax.axis_index("long"), lax.axis_index("short")
    core, chip = at_short & 1, at_short // 2
    chips = shorts // 2
    wide, heads = group_weight.shape[1], step_weight.shape[1]
    heads_here = heads // shorts
    width = heads_here * HEAD_DIM

    features = hidden_in.astype(f32)
    scaled_own = (features * mixer_gain.astype(f32)).astype(bf16)
    payload = with_square(scaled_own, jnp.sum(features * features, axis=1))
    blocks = exchanged(payload, "long")
    small, spread = call(
        functools.partial(spread_body, own, wide, heads),
        "spread",
        [at_long],
        [*blocks, group_weight, step_weight.T],
        [((rows, wide + 128), f32), ((longs, 2 * rows, 2 * own), bf16)],
        2 * rows * longs * own * (wide + heads + 1024),
    )
    small = total_over(small, "short")
    inverse = lax.rsqrt(small[:, -1:] / WIDTH + epsilon)
    group_raw = small[:, :wide] * inverse
    step_raw = lax.dynamic_slice_in_dim(small, wide + at_short * heads_here, heads_here, 1) * inverse

    mine, other = call(
        functools.partial(gates_body, own, width),
        "gates",
        [at_long, chip, core],
        [spread],
        [((chips, 2, rows, width), f32), ((chips, 2, rows, width), bf16)],
        2 * 128 * gate_in_weight.size,
        gate_in_weight,
        [
            pltpu.VMEM(gate_in_weight.shape, bf16),
            pltpu.VMEM((shorts, 2 * rows, width), f32),
            pltpu.SemaphoreType.DMA((2 * longs,)),
        ],
        46 * MIB,
    )
    mine = mine + swap(other, "short", 1).astype(f32)
    gate_in = mine[0]
    for q in range(1, chips):
        gate_in = gate_in + swap(mine[q].astype(bf16), "short", 2 * q).astype(f32)
    gate_in = gate_in * inverse

    group_window = jnp.concatenate([group_conv_state, group_raw[:, None, :]], axis=1)
    group_act = jax.nn.silu(jnp.sum(group_window * group_conv_weight[None], axis=1))
    group_index = at_long
    group_full = gather(group_act, "long")
    group_full = jnp.transpose(group_full, (1, 0, 2)).reshape(rows, longs * wide)
    state_in = lax.dynamic_slice_in_dim(group_full, group_index * STATE, STATE, 1)
    state_out = lax.dynamic_slice_in_dim(group_full, (GROUPS + group_index) * STATE, STATE, 1)

    step_size = jax.nn.softplus(step_raw + step_bias[None])
    decay = jnp.exp(-jnp.exp(decay_log)[None] * step_size)
    window = jnp.concatenate([conv_state, gate_in[1][:, None, :]], axis=1)
    mixer_input = jax.nn.silu(jnp.sum(window * conv_weight[None], axis=1))
    head_input = mixer_input.reshape(rows, heads_here, HEAD_DIM)
    new_state = (
        decay[:, :, None, None] * ssm_state
        + (step_size[:, :, None] * head_input)[:, :, :, None] * state_in[:, None, None, :]
    )
    readout = jnp.sum(new_state * state_out[:, None, None, :], axis=-1)
    readout = readout + skip_scale[None, :, None] * head_input
    readout = readout.reshape(rows, width) * jax.nn.silu(gate_in[0])

    unscaled = (readout * norm_gain[None]).astype(bf16)
    payload = with_square(unscaled, jnp.sum(readout * readout, axis=1))
    mixed_weight = fetched(out_weight, payload, "fetch_mixed")
    blocks = exchanged(payload, "short")
    mixed = call(
        functools.partial(out_body, own, width, INNER // GROUPS, shorts),
        "mixed",
        [at_short, at_long],
        [*blocks, mixed_weight],
        [((rows, own), f32)] + [((rows, own), bf16)] * (longs - 1),
        2 * rows * out_weight.size,
    )
    total = features + mixed[0]
    for k in range(longs - 1, 0, -1):
        total = total + swap(mixed[k], "long", k).astype(f32)
    middle = total.astype(bf16).astype(f32)

    scaled_own = (middle * mlp_gain.astype(f32)).astype(bf16)
    payload = with_square(scaled_own, jnp.sum(middle * middle, axis=1))
    upward_weight = fetched(up_weight, payload, "fetch_upward")
    blocks = exchanged(payload, "long")
    half = up_weight.shape[1] // 2
    mine, other = call(
        functools.partial(up_body, own),
        "upward",
        [at_long, core],
        [*blocks, upward_weight],
        [((rows, half + 128), f32), ((rows, half + 128), bf16)],
        2 * rows * up_weight.size,
    )

    def added(to, arrived):
        square = to[:, half:] + square_of(arrived[:, half:])[:, None]
        return jnp.concatenate([to[:, :half] + arrived[:, :half].astype(f32), square], axis=1)

    upward = added(mine, swap(other, "short", 1))
    sent = with_square(upward[:, :half].astype(bf16), upward[:, half])
    downward_weight = fetched(down_weight, sent, "fetch_downward")
    for k in range(1, chips):
        arrived, downward_weight = lax.optimization_barrier((swap(sent, "short", 2 * k), downward_weight))
        upward = added(upward, arrived)
    inverse_mid = lax.rsqrt(upward[:, half:][:, :1] / WIDTH + epsilon)
    active = jnp.square(jnp.maximum(upward[:, :half] * inverse_mid, 0.0)).astype(bf16)
    parts = call(
        functools.partial(down_body, own),
        "downward",
        [core, at_long],
        [active, swap(active, "short", 1), downward_weight],
        [((rows, own), f32)] + [((rows, own), bf16)] * (longs - 1),
        2 * rows * down_weight.size,
    )
    total = middle + parts[0]
    for k in range(longs - 1, 0, -1):
        total = total + swap(parts[k], "long", k).astype(f32)
    return (total.astype(bf16), new_state, window[:, 1:], group_window[:, 1:])


def solution(mesh):
    whole_groups = mesh.shape["long"] == GROUPS and mesh.shape["short"] == 4
    placed = (
        P("groups", ("short", "long")),
        P(("short", "long")),
        P(("short", "long")),
        P("short", None, "long"),
        P("short", "long"),
        P("short", "long"),
        P(("long", "short")),
        P(("long", "short")),
        P(("long", "short")),
        P(None, ("long", "short")),
        P(None, "long"),
        P("groups", None, ("long", "short")),
        P("groups", None, "long"),
        P("groups", ("long", "short"), None, None),
        P(("long", "short")),
        P("long", "short"),
        P("short", "long"),
        P("long", "short"),
    )
    return jax.shard_map(
        fast if whole_groups else local,
        mesh=mesh,
        in_specs=placed,
        out_specs=(
            P("groups", ("short", "long")),
            P("groups", ("long", "short"), None, None),
            P("groups", None, ("long", "short")),
            P("groups", None, "long"),
        ),
        check_vma=False,
    )
```

```python
import functools

import jax
import jax.numpy as jnp
from jax import lax
from jax.experimental import pallas as pl
from jax.experimental.pallas import tpu as pltpu
from jax.sharding import PartitionSpec as P

WIDTH = 8192
HEADS = 128
HEAD_DIM = 64
STATE = 128
GROUPS = 4
INNER = 8192

f32 = jnp.float32
bf16 = jnp.bfloat16
epsilon = 1e-05


def swap(value, axis, bits):
    size = lax.axis_size(axis)
    return lax.ppermute(value, axis, [(i, i ^ bits) for i in range(size)])


def in_order(blocks, index):
    stacked = jnp.stack(blocks)
    bit = 1
    while bit < len(blocks):
        shape = stacked.shape
        paired = stacked.reshape((-1, 2, bit) + shape[1:])
        stacked = jnp.where((index & bit) != 0, paired[:, ::-1], paired).reshape(shape)
        bit *= 2
    return stacked


def gather(value, axis):
    size = lax.axis_size(axis)
    blocks = [value] + [swap(value, axis, k) for k in range(1, size)]
    return in_order(blocks, lax.axis_index(axis))


def scatter_sum(parts, axis):
    size = lax.axis_size(axis)
    index = lax.axis_index(axis)
    total = lax.dynamic_index_in_dim(parts, index, 0, False)
    sent = parts.astype(bf16)
    for k in range(size - 1, 0, -1):
        block = lax.dynamic_index_in_dim(sent, index ^ k, 0, False)
        total = total + swap(block, axis, k).astype(f32)
    return total


def chip_scatter_sum(parts, axis):
    size = lax.axis_size(axis)
    index = lax.axis_index(axis)
    parts = parts.reshape((size // 2, 2) + parts.shape[1:])
    mine = lax.dynamic_index_in_dim(parts, index & 1, 1, False)
    other = lax.dynamic_index_in_dim(parts, (index & 1) ^ 1, 1, False)
    parts = mine + swap(other.astype(bf16), axis, 1).astype(f32)
    total = lax.dynamic_index_in_dim(parts, index // 2, 0, False)
    sent = parts.astype(bf16)
    for k in range(size // 2 - 1, 0, -1):
        block = lax.dynamic_index_in_dim(sent, (index // 2) ^ k, 0, False)
        total = total + swap(block, axis, 2 * k).astype(f32)
    return total


def total_over(value, axis):
    bit = 1
    while bit < lax.axis_size(axis):
        value = value + swap(value, axis, bit)
        bit *= 2
    return value


def split_pair(value):
    high = value.astype(bf16)
    return high, (value - high.astype(f32)).astype(bf16)


def with_square(block, square):
    high, low = split_pair(square)
    rows = block.shape[0]
    lanes = lax.broadcasted_iota(jnp.int32, (rows, 128), 1)
    tail = jnp.where(lanes == 0, high[:, None], jnp.where(lanes == 1, low[:, None], 0))
    return jnp.concatenate([block, tail.astype(bf16)], axis=1)


def square_of(tail):
    return tail[..., 0].astype(f32) + tail[..., 1].astype(f32)


def local(
    hidden_in,
    mixer_gain,
    mlp_gain,
    gate_in_weight,
    group_weight,
    step_weight,
    step_bias,
    decay_log,
    skip_scale,
    conv_weight,
    group_conv_weight,
    conv_state,
    group_conv_state,
    ssm_state,
    norm_gain,
    out_weight,
    up_weight,
    down_weight,
):
    rows = hidden_in.shape[0]
    longs, shorts = lax.axis_size("long"), lax.axis_size("short")
    at_long, at_short = lax.axis_index("long"), lax.axis_index("short")
    own = hidden_in.shape[1]

    features = hidden_in.astype(f32)
    scaled_own = (features * mixer_gain.astype(f32)).astype(bf16)
    blocks = gather(with_square(scaled_own, jnp.sum(features * features, axis=1)), "long")
    scaled = jnp.transpose(blocks[:, :, :own], (1, 0, 2)).reshape(rows, longs * own)
    square = jnp.sum(square_of(blocks[:, :, own:]), axis=0)

    part_groups = jnp.dot(scaled, group_weight, preferred_element_type=f32)
    part_steps = jnp.dot(scaled, step_weight, preferred_element_type=f32)
    small = total_over(jnp.concatenate([part_groups, part_steps, square[:, None]], axis=1), "short")
    wide = part_groups.shape[1]
    inverse = lax.rsqrt(small[:, -1:] / WIDTH + epsilon)
    group_raw = small[:, :wide] * inverse
    steps_here = part_steps.shape[1] // shorts
    step_raw = lax.dynamic_slice_in_dim(small, wide + at_short * steps_here, steps_here, 1) * inverse

    part_gates = jnp.einsum("rd,dkc->krc", scaled, gate_in_weight, preferred_element_type=f32)
    mixed_width = part_gates.shape[2] // shorts
    part_gates = jnp.transpose(part_gates.reshape(2, rows, shorts, mixed_width), (2, 0, 1, 3))
    gate_in = chip_scatter_sum(part_gates, "short") * inverse

    group_window = jnp.concatenate([group_conv_state, group_raw[:, None, :]], axis=1)
    group_act = jax.nn.silu(jnp.sum(group_window * group_conv_weight[None], axis=1))
    heads_here = mixed_width // HEAD_DIM
    first_head = (at_long * shorts + at_short) * heads_here
    group_index = first_head // (HEADS // GROUPS)
    group_full = gather(group_act, "long")
    group_full = jnp.transpose(group_full, (1, 0, 2)).reshape(rows, longs * wide)
    state_in = lax.dynamic_slice_in_dim(group_full, group_index * STATE, STATE, 1)
    state_out = lax.dynamic_slice_in_dim(group_full, (GROUPS + group_index) * STATE, STATE, 1)

    step_size = jax.nn.softplus(step_raw + step_bias[None])
    decay = jnp.exp(-jnp.exp(decay_log)[None] * step_size)
    window = jnp.concatenate([conv_state, gate_in[1][:, None, :]], axis=1)
    mixer_input = jax.nn.silu(jnp.sum(window * conv_weight[None], axis=1))
    head_input = mixer_input.reshape(rows, heads_here, HEAD_DIM)
    new_state = (
        decay[:, :, None, None] * ssm_state
        + (step_size[:, :, None] * head_input)[:, :, :, None] * state_in[:, None, None, :]
    )
    readout = jnp.sum(new_state * state_out[:, None, None, :], axis=-1)
    readout = readout + skip_scale[None, :, None] * head_input
    readout = readout.reshape(rows, heads_here * HEAD_DIM) * jax.nn.silu(gate_in[0])

    local_square = jnp.sum(readout * readout, axis=1)
    unscaled = (readout * norm_gain[None]).astype(bf16)
    blocks = gather(with_square(unscaled, local_square), "short")
    wide_own = unscaled.shape[1]
    normed = jnp.transpose(blocks[:, :, :wide_own], (1, 0, 2)).reshape(rows, shorts * wide_own)
    group_square = jnp.sum(square_of(blocks[:, :, wide_own:]), axis=0)
    if longs > GROUPS:
        mine = jnp.arange(GROUPS) == group_index
        totals = lax.psum(jnp.where(mine[None], group_square[:, None], 0.0), "long")
        group_square = jnp.sum(jnp.where(mine[None], totals, 0.0), axis=1)
    group_scale = lax.rsqrt(group_square / (INNER // GROUPS) + epsilon)
    part_mixed = jnp.dot(normed, out_weight, preferred_element_type=f32) * group_scale[:, None]
    part_mixed = jnp.transpose(part_mixed.reshape(rows, longs, own), (1, 0, 2))
    middle_own = (features + scatter_sum(part_mixed, "long")).astype(bf16)
    middle = middle_own.astype(f32)

    scaled_own = (middle * mlp_gain.astype(f32)).astype(bf16)
    blocks = gather(with_square(scaled_own, jnp.sum(middle * middle, axis=1)), "long")
    scaled_mid = jnp.transpose(blocks[:, :, :own], (1, 0, 2)).reshape(rows, longs * own)
    middle_square = jnp.sum(square_of(blocks[:, :, own:]), axis=0)

    part_up = jnp.dot(scaled_mid, up_weight, preferred_element_type=f32)
    half = part_up.shape[1] // 2
    core = at_short & 1
    mine = lax.dynamic_slice_in_dim(part_up, core * half, half, 1)
    other = lax.dynamic_slice_in_dim(part_up, (core ^ 1) * half, half, 1).astype(bf16)
    arrived = swap(with_square(other, middle_square), "short", 1)
    upward = mine + arrived[:, :half].astype(f32)
    middle_square = middle_square + square_of(arrived[:, half:])
    sent = with_square(upward.astype(bf16), middle_square)
    for k in range(1, shorts // 2):
        arrived = swap(sent, "short", 2 * k)
        upward = upward + arrived[:, :half].astype(f32)
        middle_square = middle_square + square_of(arrived[:, half:])
    inverse_mid = lax.rsqrt(middle_square / WIDTH + epsilon)[:, None]
    active_half = jnp.square(jnp.maximum(upward * inverse_mid, 0.0)).astype(bf16)
    pair = in_order([active_half, swap(active_half, "short", 1)], core)
    active = jnp.concatenate([pair[0], pair[1]], axis=1)

    part_down = jnp.dot(active, down_weight, preferred_element_type=f32)
    part_down = jnp.transpose(part_down.reshape(rows, longs, own), (1, 0, 2))
    hidden_out = (middle + scatter_sum(part_down, "long")).astype(bf16)
    return (hidden_out, new_state, window[:, 1:], group_window[:, 1:])


IN_VMEM = pl.BlockSpec(memory_space=pltpu.VMEM)
IN_PLACE = pl.BlockSpec(memory_space=pl.ANY)
IN_SMEM = pl.BlockSpec(memory_space=pltpu.SMEM)
MIB = 1 << 20


def cost_of(reads, flops):
    return pl.CostEstimate(flops=flops, bytes_accessed=reads, transcendentals=0)


def call(body, name, places, arrays, outs, flops, weight=None, scratch=(), room=8 * MIB):
    given = [*arrays] if weight is None else [*arrays, weight]
    reads = sum(a.size * a.dtype.itemsize for a in given)
    return pl.pallas_call(
        body,
        in_specs=[IN_SMEM] + [IN_VMEM] * len(arrays) + [IN_PLACE] * (weight is not None),
        out_specs=[IN_VMEM] * len(outs),
        out_shape=[jax.ShapeDtypeStruct(shape, dtype) for shape, dtype in outs],
        scratch_shapes=list(scratch),
        compiler_params=pltpu.CompilerParams(vmem_limit_bytes=room),
        cost_estimate=cost_of(reads, flops),
        name=name,
    )(jnp.stack(places).astype(jnp.int32), *given)


def started(copies):
    copies = [pltpu.make_async_copy(*copy) for copy in copies]
    for copy in copies:
        copy.start()
    return copies


def fetch_body(pieces, source, target, semaphores):
    step = source.shape[0] // pieces
    copies = [
        pltpu.make_async_copy(source.at[pl.ds(i * step, step)], target.at[pl.ds(i * step, step)], semaphores.at[i])
        for i in range(pieces)
    ]
    for copy in copies:
        copy.start()
    for copy in copies:
        copy.wait()


def fetched(weight, after, name, pieces=8):
    weight, _ = lax.optimization_barrier((weight, after))
    return pl.pallas_call(
        functools.partial(fetch_body, pieces),
        in_specs=[pl.BlockSpec(memory_space=pl.ANY)],
        out_specs=IN_VMEM,
        out_shape=jax.ShapeDtypeStruct(weight.shape, weight.dtype),
        scratch_shapes=[pltpu.SemaphoreType.DMA((pieces,))],
        compiler_params=pltpu.CompilerParams(vmem_limit_bytes=(34 if weight.size > 6 * MIB else 34) * MIB),
        cost_estimate=cost_of(2 * weight.size * weight.dtype.itemsize, 0),
        name=name,
    )(weight)


def two_columns(square):
    high, low = split_pair(square)
    lanes = lax.broadcasted_iota(jnp.int32, (square.shape[0], 128), 1)
    return jnp.where(lanes == 0, high.astype(f32), jnp.where(lanes == 1, low.astype(f32), 0.0)).astype(bf16)


def from_two(tail):
    return jnp.sum(tail[:, :2].astype(f32), axis=1, keepdims=True)


def spread_body(own, wide, heads, place, *refs):
    count = len(refs) - 4
    blocks, group_w, step_w, small, spread = refs[:count], refs[-4], refs[-3], refs[-2], refs[-1]
    rows = small.shape[0]
    index = place[0]
    groups = jnp.zeros((rows, wide), f32)
    steps = jnp.zeros((rows, heads), f32)
    square = jnp.zeros((rows, 1), f32)
    piece = 256
    unit = lax.broadcasted_iota(jnp.int32, (piece, 2 * piece), 0) * 2
    target = lax.broadcasted_iota(jnp.int32, (piece, 2 * piece), 1)
    for k in range(count):
        block = blocks[k][:, :own]
        start = pl.multiple_of((index ^ k) * own, own)
        groups += jnp.dot(block, group_w[pl.ds(start, own), :], preferred_element_type=f32)
        steps += lax.dot_general(
            block, step_w[:, pl.ds(start, own)], (((1,), (1,)), ((), ())), preferred_element_type=f32
        )
        square += from_two(blocks[k][:, own:])
    small[:, :wide] = groups
    lanes = lax.broadcasted_iota(jnp.int32, (rows, 128), 1)
    small[:, wide:] = jnp.where(lanes == 127, square, 0.0)
    small[:, wide : wide + heads] = steps
    for which in range(2):
        ones = (unit + which == target).astype(bf16)
        for k in range(count):
            for j in range(own // piece):
                part = jnp.dot(blocks[k][:, j * piece : (j + 1) * piece], ones, preferred_element_type=f32)
                spread[k, which * rows : (which + 1) * rows, 2 * j * piece : 2 * (j + 1) * piece] = part.astype(bf16)


def gates_body(own, width, place, spread, weight, mine, other, held, total, arrived):
    index, chip, core = place[0], place[1], place[2]
    count, rows = spread.shape[0], spread.shape[1] // 2
    piece = own // 2
    copies = started(
        (
            weight.at[pl.ds(pl.multiple_of((index ^ (i // 2)) * own + (i % 2) * piece, piece), piece)],
            held.at[pl.ds(i * piece, piece)],
            arrived.at[i],
        )
        for i in range(2 * count)
    )
    for i in range(2 * count):
        copies[i].wait()
        block = spread[i // 2, :, (i % 2) * 2 * piece : (i % 2 + 1) * 2 * piece]
        for t in range(2 * mine.shape[0]):
            side, q = divmod(t, mine.shape[0])
            column = pl.multiple_of((((chip ^ q) * 2) + (core ^ (1 - side))) * width, width)
            rows_of = held[i * piece : (i + 1) * piece, :, pl.ds(column, width)].reshape(2 * piece, width)
            value = jnp.dot(block, rows_of, preferred_element_type=f32)
            if i > 0:
                value += total[t]
            if i < 2 * count - 1:
                total[t] = value
                continue
            to = mine if side else other
            to[q, 0] = value[:rows].astype(to.dtype)
            to[q, 1] = value[rows:].astype(to.dtype)


def out_body(own, width, mean_over, count, place, *refs):
    blocks, weight, outs = refs[:count], refs[count], refs[count + 1 :]
    at_short, at_long = place[0], place[1]
    square = from_two(blocks[0][:, width:])
    for k in range(1, count):
        square += from_two(blocks[k][:, width:])
    scale = lax.rsqrt(square / mean_over + epsilon)
    for q in range(len(outs) - 1, -1, -1):
        column = pl.multiple_of((at_long ^ q) * own, own)
        total = jnp.zeros(outs[q].shape, f32)
        for k in range(count):
            start = pl.multiple_of((at_short ^ k) * width, width)
            total += jnp.dot(
                blocks[k][:, :width], weight[pl.ds(start, width), pl.ds(column, own)], preferred_element_type=f32
            )
        outs[q][...] = (total * scale).astype(outs[q].dtype)


def up_body(own, place, *refs):
    count = len(refs) - 3
    blocks, weight, mine, other = refs[:count], refs[-3], refs[-2], refs[-1]
    index, core = place[0], place[1]
    half = weight.shape[1] // 2
    piece = 512
    square = from_two(blocks[0][:, own:])
    for k in range(1, count):
        square += from_two(blocks[k][:, own:])
    for side in range(2):
        for j in range(half // piece):
            column = pl.multiple_of((core ^ (1 - side)) * half + j * piece, piece)
            total = jnp.zeros((mine.shape[0], piece), f32)
            for k in range(count):
                start = pl.multiple_of((index ^ k) * own, own)
                total += jnp.dot(
                    blocks[k][:, :own], weight[pl.ds(start, own), pl.ds(column, piece)], preferred_element_type=f32
                )
            if side == 0:
                other[:, j * piece : (j + 1) * piece] = total.astype(bf16)
            else:
                mine[:, j * piece : (j + 1) * piece] = total
    other[:, half:] = two_columns(square)
    mine[:, half:] = jnp.broadcast_to(square, (square.shape[0], 128))


def down_body(own, place, first, second, weight, *outs):
    core, at_long = place[0], place[1]
    half = first.shape[1]
    for q in range(len(outs) - 1, -1, -1):
        column = pl.multiple_of((at_long ^ q) * own, own)
        total = jnp.zeros(outs[q].shape, f32)
        for k, block in enumerate((first, second)):
            start = pl.multiple_of((core ^ k) * half, half)
            total += jnp.dot(block[...], weight[pl.ds(start, half), pl.ds(column, own)], preferred_element_type=f32)
        outs[q][...] = total.astype(outs[q].dtype)


def product_body(step, state, out_hi, out_lo, result, held, arrived):
    rows, heads, size, entries = state.shape

    def copy_of(i):
        block = pl.ds(i * step, step)
        return pltpu.make_async_copy(state.at[block], held.at[block], arrived.at[i])

    for i in range(rows // step):
        copy_of(i).start()

    def one_block(i, carry):
        copy_of(i).wait()
        base = pl.multiple_of(i * step, step)
        left = jnp.concatenate([out_hi[pl.ds(base, step), :], out_lo[pl.ds(base, step), :]], axis=0)
        left = jnp.concatenate([left, left], axis=1).astype(bf16)
        lines = []
        for r in range(step):
            block = held[base + r].reshape(heads * size, entries)
            high = block.astype(bf16)
            low = (block - high.astype(f32)).astype(bf16)
            value = lax.dot_general(
                left, jnp.concatenate([high, low], axis=1), (((1,), (1,)), ((), ())), preferred_element_type=f32
            )
            lines.append(value[r : r + 1] + value[step + r : step + r + 1])
        result[pl.ds(base, step), :] = jnp.concatenate(lines, axis=0)
        return carry

    lax.fori_loop(0, rows // step, one_block, 0)


def state_products(state, state_out):
    rows, heads, size, entries = state.shape
    step = 8
    high, low = split_pair(state_out)
    return pl.pallas_call(
        functools.partial(product_body, step),
        in_specs=[IN_PLACE, IN_VMEM, IN_VMEM],
        out_specs=IN_VMEM,
        out_shape=jax.ShapeDtypeStruct((rows, heads * size), f32),
        scratch_shapes=[pltpu.VMEM(state.shape, f32), pltpu.SemaphoreType.DMA((rows // step,))],
        compiler_params=pltpu.CompilerParams(vmem_limit_bytes=46 * MIB),
        cost_estimate=cost_of(state.size * 4, 64 * state.size),
        name="state_products",
    )(state, high.astype(f32), low.astype(f32))


def update_body(first, rows, decay, state, inputs, state_in, *refs):
    target, held, across, arrived, sent = refs[-5:]
    _, heads, size, _ = state.shape
    step, together = 4, 4
    pieces = rows // step
    come = started(
        (state.at[pl.ds(first + i * step, step)], held.at[pl.ds(i * step, step)], arrived.at[i]) for i in range(pieces)
    )
    across[...] = inputs[...].T
    go = []
    for i in range(pieces):
        come[i].wait()

        def some_heads(g, carry, i=i):
            for t in range(together):
                h = g * together + t
                block = across[pl.ds(pl.multiple_of(h * size, size), size), first + i * step : first + (i + 1) * step]
                for j in range(step):
                    r = i * step + j
                    scaled = held[r, h] * decay[(first + r) * heads + h]
                    held[r, h] = scaled + block[:, j : j + 1] * state_in[r : r + 1, :]
            return carry

        lax.fori_loop(0, heads // together, some_heads, 0)
        go += started([(held.at[pl.ds(i * step, step)], target.at[pl.ds(first + i * step, step)], sent.at[i])])
    for copy in go:
        copy.wait()


def updated(state, decay, inputs, state_in, first, rows, before, after, name):
    state, _ = lax.optimization_barrier((state, after))
    given = [decay.reshape(-1), state, inputs, state_in[first : first + rows]]
    specs = [IN_SMEM, IN_PLACE, IN_VMEM, IN_VMEM]
    if before is not None:
        given.append(before)
        specs.append(IN_PLACE)
    pieces = rows // 4
    return pl.pallas_call(
        functools.partial(update_body, first, rows),
        in_specs=specs,
        out_specs=IN_PLACE,
        out_shape=jax.ShapeDtypeStruct(state.shape, f32),
        scratch_shapes=[
            pltpu.VMEM((rows,) + state.shape[1:], f32),
            pltpu.VMEM(inputs.shape[::-1], f32),
            pltpu.SemaphoreType.DMA((pieces,)),
            pltpu.SemaphoreType.DMA((pieces,)),
        ],
        input_output_aliases={} if before is None else {4: 0},
        compiler_params=pltpu.CompilerParams(vmem_limit_bytes=40 * MIB),
        cost_estimate=cost_of(8 * rows * state[0].size, 3 * rows * state[0].size),
        name=name,
    )(*given)


def exchanged(value, axis):
    return [value] + [swap(value, axis, k) for k in range(1, lax.axis_size(axis))]


def fast(
    hidden_in,
    mixer_gain,
    mlp_gain,
    gate_in_weight,
    group_weight,
    step_weight,
    step_bias,
    decay_log,
    skip_scale,
    conv_weight,
    group_conv_weight,
    conv_state,
    group_conv_state,
    ssm_state,
    norm_gain,
    out_weight,
    up_weight,
    down_weight,
):
    rows, own = hidden_in.shape
    longs, shorts = lax.axis_size("long"), lax.axis_size("short")
    at_long, at_short = lax.axis_index("long"), lax.axis_index("short")
    core, chip = at_short & 1, at_short // 2
    chips = shorts // 2
    wide, heads = group_weight.shape[1], step_weight.shape[1]
    heads_here = heads // shorts
    width = heads_here * HEAD_DIM

    features = hidden_in.astype(f32)
    scaled_own = (features * mixer_gain.astype(f32)).astype(bf16)
    payload = with_square(scaled_own, jnp.sum(features * features, axis=1))
    blocks = exchanged(payload, "long")
    small, spread = call(
        functools.partial(spread_body, own, wide, heads),
        "spread",
        [at_long],
        [*blocks, fetched(group_weight, payload, "fetch_groups", 2), fetched(step_weight.T, payload, "fetch_steps", 1)],
        [((rows, wide + 128), f32), ((longs, 2 * rows, 2 * own), bf16)],
        2 * rows * longs * own * (wide + heads + 1024),
    )
    small = total_over(small, "short")
    inverse = lax.rsqrt(small[:, -1:] / WIDTH + epsilon)
    group_raw = small[:, :wide] * inverse
    step_raw = lax.dynamic_slice_in_dim(small, wide + at_short * heads_here, heads_here, 1) * inverse

    mine, other = call(
        functools.partial(gates_body, own, width),
        "gates",
        [at_long, chip, core],
        [spread],
        [((chips, 2, rows, width), f32), ((chips, 2, rows, width), bf16)],
        2 * 128 * gate_in_weight.size,
        gate_in_weight,
        [
            pltpu.VMEM(gate_in_weight.shape, bf16),
            pltpu.VMEM((shorts, 2 * rows, width), f32),
            pltpu.SemaphoreType.DMA((2 * longs,)),
        ],
        46 * MIB,
    )
    mine = mine + swap(other, "short", 1).astype(f32)
    gate_in = mine[0]
    for q in range(1, chips):
        gate_in = gate_in + swap(mine[q].astype(bf16), "short", 2 * q).astype(f32)
    gate_in = gate_in * inverse

    group_window = jnp.concatenate([group_conv_state, group_raw[:, None, :]], axis=1)
    group_act = jax.nn.silu(jnp.sum(group_window * group_conv_weight[None], axis=1))
    low, high = group_act[:, :STATE], group_act[:, STATE:]
    one = lax.ppermute(jnp.where(at_long < 2, high, low), "long", [(0, 1), (1, 3), (2, 0), (3, 2)])
    two = lax.ppermute(jnp.where(at_long == 1, low, high), "long", [(1, 2), (2, 1)])
    state_in = jnp.where(at_long == 0, low, jnp.where(at_long == 2, two, one))
    state_out = jnp.where(at_long == 3, high, jnp.where(at_long == 1, two, one))
    products = state_products(ssm_state, state_out)

    step_size = jax.nn.softplus(step_raw + step_bias[None])
    decay = jnp.exp(-jnp.exp(decay_log)[None] * step_size)
    window = jnp.concatenate([conv_state, gate_in[1][:, None, :]], axis=1)
    mixer_input = jax.nn.silu(jnp.sum(window * conv_weight[None], axis=1))
    inputs = jnp.repeat(step_size, HEAD_DIM, axis=1) * mixer_input
    readout = jnp.repeat(decay, HEAD_DIM, axis=1) * products
    readout = readout + inputs * jnp.sum(state_in * state_out, axis=1, keepdims=True)
    readout = readout + jnp.repeat(skip_scale, HEAD_DIM)[None] * mixer_input
    readout = readout * jax.nn.silu(gate_in[0])

    unscaled = (readout * norm_gain[None]).astype(bf16)
    payload = with_square(unscaled, jnp.sum(readout * readout, axis=1))
    mixed_weight = fetched(out_weight, payload, "fetch_mixed")
    blocks = exchanged(payload, "short")
    mixed = call(
        functools.partial(out_body, own, width, INNER // GROUPS, shorts),
        "mixed",
        [at_short, at_long],
        [*blocks, mixed_weight],
        [((rows, own), f32)] + [((rows, own), bf16)] * (longs - 1),
        2 * rows * out_weight.size,
    )
    half_rows = rows // 2
    new_state = updated(ssm_state, decay, inputs, state_in, 0, half_rows, None, mixed[-1], "update_first")
    arrived = [swap(mixed[k], "long", k) for k in range(longs - 1, 0, -1)]
    *arrived, new_state = lax.optimization_barrier((*arrived, new_state))
    total = features + mixed[0]
    for block in arrived:
        total = total + block.astype(f32)
    middle = total.astype(bf16).astype(f32)

    scaled_own = (middle * mlp_gain.astype(f32)).astype(bf16)
    payload = with_square(scaled_own, jnp.sum(middle * middle, axis=1))
    upward_weight = fetched(up_weight, payload, "fetch_upward")
    blocks = exchanged(payload, "long")
    half = up_weight.shape[1] // 2
    mine, other = call(
        functools.partial(up_body, own),
        "upward",
        [at_long, core],
        [*blocks, upward_weight],
        [((rows, half + 128), f32), ((rows, half + 128), bf16)],
        2 * rows * up_weight.size,
    )

    def added(to, arrived):
        square = to[:, half:] + square_of(arrived[:, half:])[:, None]
        return jnp.concatenate([to[:, :half] + arrived[:, :half].astype(f32), square], axis=1)

    upward = added(mine, swap(other, "short", 1))
    sent = with_square(upward[:, :half].astype(bf16), upward[:, half])
    downward_weight = fetched(down_weight, sent, "fetch_downward")
    for k in range(1, chips):
        arrived, downward_weight = lax.optimization_barrier((swap(sent, "short", 2 * k), downward_weight))
        upward = added(upward, arrived)
    inverse_mid = lax.rsqrt(upward[:, half:][:, :1] / WIDTH + epsilon)
    active = jnp.square(jnp.maximum(upward[:, :half] * inverse_mid, 0.0)).astype(bf16)
    parts = call(
        functools.partial(down_body, own),
        "downward",
        [core, at_long],
        [active, swap(active, "short", 1), downward_weight],
        [((rows, own), f32)] + [((rows, own), bf16)] * (longs - 1),
        2 * rows * down_weight.size,
    )
    new_state = updated(ssm_state, decay, inputs, state_in, half_rows, rows - half_rows, new_state, parts[-1], "update_last")
    arrived = [swap(parts[k], "long", k) for k in range(longs - 1, 0, -1)]
    *arrived, new_state = lax.optimization_barrier((*arrived, new_state))
    total = middle + parts[0]
    for block in arrived:
        total = total + block.astype(f32)
    return (total.astype(bf16), new_state, window[:, 1:], group_window[:, 1:])


def solution(mesh):
    whole_groups = mesh.shape["long"] == GROUPS and mesh.shape["short"] == 4
    placed = (
        P("groups", ("short", "long")),
        P(("short", "long")),
        P(("short", "long")),
        P("short", None, "long"),
        P("short", "long"),
        P("short", "long"),
        P(("long", "short")),
        P(("long", "short")),
        P(("long", "short")),
        P(None, ("long", "short")),
        P(None, "long"),
        P("groups", None, ("long", "short")),
        P("groups", None, "long"),
        P("groups", ("long", "short"), None, None),
        P(("long", "short")),
        P("long", "short"),
        P("short", "long"),
        P("long", "short"),
    )
    return jax.shard_map(
        fast if whole_groups else local,
        mesh=mesh,
        in_specs=placed,
        out_specs=(
            P("groups", ("short", "long")),
            P("groups", ("long", "short"), None, None),
            P("groups", None, ("long", "short")),
            P("groups", None, "long"),
        ),
        check_vma=False,
    )
```

```python
import functools

import jax
import jax.numpy as jnp
from jax import lax
from jax.experimental import pallas as pl
from jax.experimental.pallas import tpu as pltpu
from jax.sharding import PartitionSpec as P

WIDTH = 8192
HEADS = 128
HEAD_DIM = 64
STATE = 128
GROUPS = 4
INNER = 8192

f32 = jnp.float32
bf16 = jnp.bfloat16
epsilon = 1e-05


def swap(value, axis, bits):
    size = lax.axis_size(axis)
    return lax.ppermute(value, axis, [(i, i ^ bits) for i in range(size)])


def in_order(blocks, index):
    stacked = jnp.stack(blocks)
    bit = 1
    while bit < len(blocks):
        shape = stacked.shape
        paired = stacked.reshape((-1, 2, bit) + shape[1:])
        stacked = jnp.where((index & bit) != 0, paired[:, ::-1], paired).reshape(shape)
        bit *= 2
    return stacked


def gather(value, axis):
    size = lax.axis_size(axis)
    blocks = [value] + [swap(value, axis, k) for k in range(1, size)]
    return in_order(blocks, lax.axis_index(axis))


def scatter_sum(parts, axis):
    size = lax.axis_size(axis)
    index = lax.axis_index(axis)
    total = lax.dynamic_index_in_dim(parts, index, 0, False)
    sent = parts.astype(bf16)
    for k in range(size - 1, 0, -1):
        block = lax.dynamic_index_in_dim(sent, index ^ k, 0, False)
        total = total + swap(block, axis, k).astype(f32)
    return total


def chip_scatter_sum(parts, axis):
    size = lax.axis_size(axis)
    index = lax.axis_index(axis)
    parts = parts.reshape((size // 2, 2) + parts.shape[1:])
    mine = lax.dynamic_index_in_dim(parts, index & 1, 1, False)
    other = lax.dynamic_index_in_dim(parts, (index & 1) ^ 1, 1, False)
    parts = mine + swap(other.astype(bf16), axis, 1).astype(f32)
    total = lax.dynamic_index_in_dim(parts, index // 2, 0, False)
    sent = parts.astype(bf16)
    for k in range(size // 2 - 1, 0, -1):
        block = lax.dynamic_index_in_dim(sent, (index // 2) ^ k, 0, False)
        total = total + swap(block, axis, 2 * k).astype(f32)
    return total


def total_over(value, axis):
    bit = 1
    while bit < lax.axis_size(axis):
        value = value + swap(value, axis, bit)
        bit *= 2
    return value


def split_pair(value):
    high = value.astype(bf16)
    return high, (value - high.astype(f32)).astype(bf16)


def with_square(block, square):
    high, low = split_pair(square)
    rows = block.shape[0]
    lanes = lax.broadcasted_iota(jnp.int32, (rows, 128), 1)
    tail = jnp.where(lanes == 0, high[:, None], jnp.where(lanes == 1, low[:, None], 0))
    return jnp.concatenate([block, tail.astype(bf16)], axis=1)


def square_of(tail):
    return tail[..., 0].astype(f32) + tail[..., 1].astype(f32)


def local(
    hidden_in,
    mixer_gain,
    mlp_gain,
    gate_in_weight,
    group_weight,
    step_weight,
    step_bias,
    decay_log,
    skip_scale,
    conv_weight,
    group_conv_weight,
    conv_state,
    group_conv_state,
    ssm_state,
    norm_gain,
    out_weight,
    up_weight,
    down_weight,
):
    rows = hidden_in.shape[0]
    longs, shorts = lax.axis_size("long"), lax.axis_size("short")
    at_long, at_short = lax.axis_index("long"), lax.axis_index("short")
    own = hidden_in.shape[1]

    features = hidden_in.astype(f32)
    scaled_own = (features * mixer_gain.astype(f32)).astype(bf16)
    blocks = gather(with_square(scaled_own, jnp.sum(features * features, axis=1)), "long")
    scaled = jnp.transpose(blocks[:, :, :own], (1, 0, 2)).reshape(rows, longs * own)
    square = jnp.sum(square_of(blocks[:, :, own:]), axis=0)

    part_groups = jnp.dot(scaled, group_weight, preferred_element_type=f32)
    part_steps = jnp.dot(scaled, step_weight, preferred_element_type=f32)
    small = total_over(jnp.concatenate([part_groups, part_steps, square[:, None]], axis=1), "short")
    wide = part_groups.shape[1]
    inverse = lax.rsqrt(small[:, -1:] / WIDTH + epsilon)
    group_raw = small[:, :wide] * inverse
    steps_here = part_steps.shape[1] // shorts
    step_raw = lax.dynamic_slice_in_dim(small, wide + at_short * steps_here, steps_here, 1) * inverse

    part_gates = jnp.einsum("rd,dkc->krc", scaled, gate_in_weight, preferred_element_type=f32)
    mixed_width = part_gates.shape[2] // shorts
    part_gates = jnp.transpose(part_gates.reshape(2, rows, shorts, mixed_width), (2, 0, 1, 3))
    gate_in = chip_scatter_sum(part_gates, "short") * inverse

    group_window = jnp.concatenate([group_conv_state, group_raw[:, None, :]], axis=1)
    group_act = jax.nn.silu(jnp.sum(group_window * group_conv_weight[None], axis=1))
    heads_here = mixed_width // HEAD_DIM
    first_head = (at_long * shorts + at_short) * heads_here
    group_index = first_head // (HEADS // GROUPS)
    group_full = gather(group_act, "long")
    group_full = jnp.transpose(group_full, (1, 0, 2)).reshape(rows, longs * wide)
    state_in = lax.dynamic_slice_in_dim(group_full, group_index * STATE, STATE, 1)
    state_out = lax.dynamic_slice_in_dim(group_full, (GROUPS + group_index) * STATE, STATE, 1)

    step_size = jax.nn.softplus(step_raw + step_bias[None])
    decay = jnp.exp(-jnp.exp(decay_log)[None] * step_size)
    window = jnp.concatenate([conv_state, gate_in[1][:, None, :]], axis=1)
    mixer_input = jax.nn.silu(jnp.sum(window * conv_weight[None], axis=1))
    head_input = mixer_input.reshape(rows, heads_here, HEAD_DIM)
    new_state = (
        decay[:, :, None, None] * ssm_state
        + (step_size[:, :, None] * head_input)[:, :, :, None] * state_in[:, None, None, :]
    )
    readout = jnp.sum(new_state * state_out[:, None, None, :], axis=-1)
    readout = readout + skip_scale[None, :, None] * head_input
    readout = readout.reshape(rows, heads_here * HEAD_DIM) * jax.nn.silu(gate_in[0])

    local_square = jnp.sum(readout * readout, axis=1)
    unscaled = (readout * norm_gain[None]).astype(bf16)
    blocks = gather(with_square(unscaled, local_square), "short")
    wide_own = unscaled.shape[1]
    normed = jnp.transpose(blocks[:, :, :wide_own], (1, 0, 2)).reshape(rows, shorts * wide_own)
    group_square = jnp.sum(square_of(blocks[:, :, wide_own:]), axis=0)
    if longs > GROUPS:
        mine = jnp.arange(GROUPS) == group_index
        totals = lax.psum(jnp.where(mine[None], group_square[:, None], 0.0), "long")
        group_square = jnp.sum(jnp.where(mine[None], totals, 0.0), axis=1)
    group_scale = lax.rsqrt(group_square / (INNER // GROUPS) + epsilon)
    part_mixed = jnp.dot(normed, out_weight, preferred_element_type=f32) * group_scale[:, None]
    part_mixed = jnp.transpose(part_mixed.reshape(rows, longs, own), (1, 0, 2))
    middle_own = (features + scatter_sum(part_mixed, "long")).astype(bf16)
    middle = middle_own.astype(f32)

    scaled_own = (middle * mlp_gain.astype(f32)).astype(bf16)
    blocks = gather(with_square(scaled_own, jnp.sum(middle * middle, axis=1)), "long")
    scaled_mid = jnp.transpose(blocks[:, :, :own], (1, 0, 2)).reshape(rows, longs * own)
    middle_square = jnp.sum(square_of(blocks[:, :, own:]), axis=0)

    part_up = jnp.dot(scaled_mid, up_weight, preferred_element_type=f32)
    half = part_up.shape[1] // 2
    core = at_short & 1
    mine = lax.dynamic_slice_in_dim(part_up, core * half, half, 1)
    other = lax.dynamic_slice_in_dim(part_up, (core ^ 1) * half, half, 1).astype(bf16)
    arrived = swap(with_square(other, middle_square), "short", 1)
    upward = mine + arrived[:, :half].astype(f32)
    middle_square = middle_square + square_of(arrived[:, half:])
    sent = with_square(upward.astype(bf16), middle_square)
    for k in range(1, shorts // 2):
        arrived = swap(sent, "short", 2 * k)
        upward = upward + arrived[:, :half].astype(f32)
        middle_square = middle_square + square_of(arrived[:, half:])
    inverse_mid = lax.rsqrt(middle_square / WIDTH + epsilon)[:, None]
    active_half = jnp.square(jnp.maximum(upward * inverse_mid, 0.0)).astype(bf16)
    pair = in_order([active_half, swap(active_half, "short", 1)], core)
    active = jnp.concatenate([pair[0], pair[1]], axis=1)

    part_down = jnp.dot(active, down_weight, preferred_element_type=f32)
    part_down = jnp.transpose(part_down.reshape(rows, longs, own), (1, 0, 2))
    hidden_out = (middle + scatter_sum(part_down, "long")).astype(bf16)
    return (hidden_out, new_state, window[:, 1:], group_window[:, 1:])


IN_VMEM = pl.BlockSpec(memory_space=pltpu.VMEM)
IN_PLACE = pl.BlockSpec(memory_space=pl.ANY)
IN_SMEM = pl.BlockSpec(memory_space=pltpu.SMEM)
MIB = 1 << 20


def cost_of(reads, flops):
    return pl.CostEstimate(flops=flops, bytes_accessed=reads, transcendentals=0)


def call(body, name, places, arrays, outs, flops, weight=None, scratch=(), room=8 * MIB):
    given = [*arrays] if weight is None else [*arrays, weight]
    reads = sum(a.size * a.dtype.itemsize for a in given)
    return pl.pallas_call(
        body,
        in_specs=[IN_SMEM] + [IN_VMEM] * len(arrays) + [IN_PLACE] * (weight is not None),
        out_specs=[IN_VMEM] * len(outs),
        out_shape=[jax.ShapeDtypeStruct(shape, dtype) for shape, dtype in outs],
        scratch_shapes=list(scratch),
        compiler_params=pltpu.CompilerParams(vmem_limit_bytes=room),
        cost_estimate=cost_of(reads, flops),
        name=name,
    )(jnp.stack(places).astype(jnp.int32), *given)


def started(copies):
    copies = [pltpu.make_async_copy(*copy) for copy in copies]
    for copy in copies:
        copy.start()
    return copies


def fetch_body(pieces, source, target, semaphores):
    step = source.shape[0] // pieces
    copies = [
        pltpu.make_async_copy(source.at[pl.ds(i * step, step)], target.at[pl.ds(i * step, step)], semaphores.at[i])
        for i in range(pieces)
    ]
    for copy in copies:
        copy.start()
    for copy in copies:
        copy.wait()


def fetched(weight, after, name, pieces=8):
    weight, _ = lax.optimization_barrier((weight, after))
    return pl.pallas_call(
        functools.partial(fetch_body, pieces),
        in_specs=[pl.BlockSpec(memory_space=pl.ANY)],
        out_specs=IN_VMEM,
        out_shape=jax.ShapeDtypeStruct(weight.shape, weight.dtype),
        scratch_shapes=[pltpu.SemaphoreType.DMA((pieces,))],
        compiler_params=pltpu.CompilerParams(vmem_limit_bytes=(34 if weight.size > 6 * MIB else 34) * MIB),
        cost_estimate=cost_of(2 * weight.size * weight.dtype.itemsize, 0),
        name=name,
    )(weight)


def two_columns(square):
    high, low = split_pair(square)
    lanes = lax.broadcasted_iota(jnp.int32, (square.shape[0], 128), 1)
    return jnp.where(lanes == 0, high.astype(f32), jnp.where(lanes == 1, low.astype(f32), 0.0)).astype(bf16)


def from_two(tail):
    return jnp.sum(tail[:, :2].astype(f32), axis=1, keepdims=True)


def spread_body(own, wide, heads, place, *refs):
    count = len(refs) - 4
    blocks, group_w, step_w, small, spread = refs[:count], refs[-4], refs[-3], refs[-2], refs[-1]
    rows = small.shape[0]
    index = place[0]
    groups = jnp.zeros((rows, wide), f32)
    steps = jnp.zeros((rows, heads), f32)
    square = jnp.zeros((rows, 1), f32)
    piece = 256
    unit = lax.broadcasted_iota(jnp.int32, (piece, 2 * piece), 0) * 2
    target = lax.broadcasted_iota(jnp.int32, (piece, 2 * piece), 1)
    for k in range(count):
        block = blocks[k][:, :own]
        start = pl.multiple_of((index ^ k) * own, own)
        groups += jnp.dot(block, group_w[pl.ds(start, own), :], preferred_element_type=f32)
        steps += lax.dot_general(
            block, step_w[:, pl.ds(start, own)], (((1,), (1,)), ((), ())), preferred_element_type=f32
        )
        square += from_two(blocks[k][:, own:])
    small[:, :wide] = groups
    lanes = lax.broadcasted_iota(jnp.int32, (rows, 128), 1)
    small[:, wide:] = jnp.where(lanes == 127, square, 0.0)
    small[:, wide : wide + heads] = steps
    for which in range(2):
        ones = (unit + which == target).astype(bf16)
        for k in range(count):
            for j in range(own // piece):
                part = jnp.dot(blocks[k][:, j * piece : (j + 1) * piece], ones, preferred_element_type=f32)
                spread[k, which * rows : (which + 1) * rows, 2 * j * piece : 2 * (j + 1) * piece] = part.astype(bf16)


def gates_body(own, width, place, spread, weight, mine, other, held, total, arrived):
    index, chip, core = place[0], place[1], place[2]
    count, rows = spread.shape[0], spread.shape[1] // 2
    piece = own // 2
    copies = started(
        (
            weight.at[pl.ds(pl.multiple_of((index ^ (i // 2)) * own + (i % 2) * piece, piece), piece)],
            held.at[pl.ds(i * piece, piece)],
            arrived.at[i],
        )
        for i in range(2 * count)
    )
    for i in range(2 * count):
        copies[i].wait()
        block = spread[i // 2, :, (i % 2) * 2 * piece : (i % 2 + 1) * 2 * piece]
        for t in range(2 * mine.shape[0]):
            side, q = divmod(t, mine.shape[0])
            column = pl.multiple_of((((chip ^ q) * 2) + (core ^ (1 - side))) * width, width)
            rows_of = held[i * piece : (i + 1) * piece, :, pl.ds(column, width)].reshape(2 * piece, width)
            value = jnp.dot(block, rows_of, preferred_element_type=f32)
            if i > 0:
                value += total[t]
            if i < 2 * count - 1:
                total[t] = value
                continue
            to = mine if side else other
            to[q, 0] = value[:rows].astype(to.dtype)
            to[q, 1] = value[rows:].astype(to.dtype)


def out_body(own, width, mean_over, count, place, *refs):
    blocks, weight, outs = refs[:count], refs[count], refs[count + 1 :]
    at_short, at_long = place[0], place[1]
    square = from_two(blocks[0][:, width:])
    for k in range(1, count):
        square += from_two(blocks[k][:, width:])
    scale = lax.rsqrt(square / mean_over + epsilon)
    for q in range(len(outs) - 1, -1, -1):
        column = pl.multiple_of((at_long ^ q) * own, own)
        total = jnp.zeros(outs[q].shape, f32)
        for k in range(count):
            start = pl.multiple_of((at_short ^ k) * width, width)
            total += jnp.dot(
                blocks[k][:, :width], weight[pl.ds(start, width), pl.ds(column, own)], preferred_element_type=f32
            )
        outs[q][...] = (total * scale).astype(outs[q].dtype)


def up_body(own, place, *refs):
    count = len(refs) - 3
    blocks, weight, mine, other = refs[:count], refs[-3], refs[-2], refs[-1]
    index, core = place[0], place[1]
    half = weight.shape[1] // 2
    piece = 512
    square = from_two(blocks[0][:, own:])
    for k in range(1, count):
        square += from_two(blocks[k][:, own:])
    for side in range(2):
        for j in range(half // piece):
            column = pl.multiple_of((core ^ (1 - side)) * half + j * piece, piece)
            total = jnp.zeros((mine.shape[0], piece), f32)
            for k in range(count):
                start = pl.multiple_of((index ^ k) * own, own)
                total += jnp.dot(
                    blocks[k][:, :own], weight[pl.ds(start, own), pl.ds(column, piece)], preferred_element_type=f32
                )
            if side == 0:
                other[:, j * piece : (j + 1) * piece] = total.astype(bf16)
            else:
                mine[:, j * piece : (j + 1) * piece] = total
    other[:, half:] = two_columns(square)
    mine[:, half:] = jnp.broadcast_to(square, (square.shape[0], 128))


def down_body(own, place, first, second, weight, *outs):
    core, at_long = place[0], place[1]
    half = first.shape[1]
    for q in range(len(outs) - 1, -1, -1):
        column = pl.multiple_of((at_long ^ q) * own, own)
        total = jnp.zeros(outs[q].shape, f32)
        for k, block in enumerate((first, second)):
            start = pl.multiple_of((core ^ k) * half, half)
            total += jnp.dot(block[...], weight[pl.ds(start, half), pl.ds(column, own)], preferred_element_type=f32)
        outs[q][...] = total.astype(outs[q].dtype)


def product_body(step, state, out_hi, out_lo, result, held, arrived):
    rows, heads, size, entries = state.shape

    def copy_of(i):
        block = pl.ds(i * step, step)
        return pltpu.make_async_copy(state.at[block], held.at[block], arrived.at[i])

    for i in range(rows // step):
        copy_of(i).start()

    def one_block(i, carry):
        copy_of(i).wait()
        base = pl.multiple_of(i * step, step)
        left = jnp.concatenate([out_hi[pl.ds(base, step), :], out_lo[pl.ds(base, step), :]], axis=0)
        left = jnp.concatenate([left, left], axis=1).astype(bf16)
        lines = []
        for r in range(step):
            block = held[base + r].reshape(heads * size, entries)
            high = block.astype(bf16)
            low = (block - high.astype(f32)).astype(bf16)
            value = lax.dot_general(
                left, jnp.concatenate([high, low], axis=1), (((1,), (1,)), ((), ())), preferred_element_type=f32
            )
            lines.append(value[r : r + 1] + value[step + r : step + r + 1])
        result[pl.ds(base, step), :] = jnp.concatenate(lines, axis=0)
        return carry

    lax.fori_loop(0, rows // step, one_block, 0)


def state_products(state, state_out):
    rows, heads, size, entries = state.shape
    step = 8
    high, low = split_pair(state_out)
    return pl.pallas_call(
        functools.partial(product_body, step),
        in_specs=[IN_PLACE, IN_VMEM, IN_VMEM],
        out_specs=IN_VMEM,
        out_shape=jax.ShapeDtypeStruct((rows, heads * size), f32),
        scratch_shapes=[pltpu.VMEM(state.shape, f32), pltpu.SemaphoreType.DMA((rows // step,))],
        compiler_params=pltpu.CompilerParams(vmem_limit_bytes=46 * MIB),
        cost_estimate=cost_of(state.size * 4, 64 * state.size),
        name="state_products",
    )(state, high.astype(f32), low.astype(f32))


def update_body(first, rows, decay, state, inputs, state_in, *refs):
    target, held, across, arrived, sent = refs[-5:]
    _, heads, size, _ = state.shape
    step, together = 2, 8
    pieces = rows // step
    come = started(
        (state.at[pl.ds(first + i * step, step)], held.at[pl.ds(i * step, step)], arrived.at[i]) for i in range(pieces)
    )
    across[...] = inputs[...].T
    go = []
    for i in range(pieces):
        come[i].wait()

        def some_heads(g, carry, i=i):
            for t in range(together):
                h = g * together + t
                block = across[pl.ds(pl.multiple_of(h * size, size), size), first + i * step : first + (i + 1) * step]
                for j in range(step):
                    r = i * step + j
                    scaled = held[r, h] * decay[(first + r) * heads + h]
                    held[r, h] = scaled + block[:, j : j + 1] * state_in[r : r + 1, :]
            return carry

        lax.fori_loop(0, heads // together, some_heads, 0)
        go += started([(held.at[pl.ds(i * step, step)], target.at[pl.ds(first + i * step, step)], sent.at[i])])
    for copy in go:
        copy.wait()


def updated(state, decay, inputs, state_in, first, rows, before, after, name):
    state, _ = lax.optimization_barrier((state, after))
    given = [decay.reshape(-1), state, inputs, state_in[first : first + rows]]
    specs = [IN_SMEM, IN_PLACE, IN_VMEM, IN_VMEM]
    if before is not None:
        given.append(before)
        specs.append(IN_PLACE)
    pieces = rows // 2
    return pl.pallas_call(
        functools.partial(update_body, first, rows),
        in_specs=specs,
        out_specs=IN_PLACE,
        out_shape=jax.ShapeDtypeStruct(state.shape, f32),
        scratch_shapes=[
            pltpu.VMEM((rows,) + state.shape[1:], f32),
            pltpu.VMEM(inputs.shape[::-1], f32),
            pltpu.SemaphoreType.DMA((pieces,)),
            pltpu.SemaphoreType.DMA((pieces,)),
        ],
        input_output_aliases={} if before is None else {4: 0},
        compiler_params=pltpu.CompilerParams(vmem_limit_bytes=40 * MIB),
        cost_estimate=cost_of(8 * rows * state[0].size, 3 * rows * state[0].size),
        name=name,
    )(*given)


def exchanged(value, axis):
    return [value] + [swap(value, axis, k) for k in range(1, lax.axis_size(axis))]


def fast(
    hidden_in,
    mixer_gain,
    mlp_gain,
    gate_in_weight,
    group_weight,
    step_weight,
    step_bias,
    decay_log,
    skip_scale,
    conv_weight,
    group_conv_weight,
    conv_state,
    group_conv_state,
    ssm_state,
    norm_gain,
    out_weight,
    up_weight,
    down_weight,
):
    rows, own = hidden_in.shape
    longs, shorts = lax.axis_size("long"), lax.axis_size("short")
    at_long, at_short = lax.axis_index("long"), lax.axis_index("short")
    core, chip = at_short & 1, at_short // 2
    chips = shorts // 2
    wide, heads = group_weight.shape[1], step_weight.shape[1]
    heads_here = heads // shorts
    width = heads_here * HEAD_DIM

    features = hidden_in.astype(f32)
    scaled_own = (features * mixer_gain.astype(f32)).astype(bf16)
    payload = with_square(scaled_own, jnp.sum(features * features, axis=1))
    blocks = exchanged(payload, "long")
    small, spread = call(
        functools.partial(spread_body, own, wide, heads),
        "spread",
        [at_long],
        [*blocks, fetched(group_weight, payload, "fetch_groups", 2), fetched(step_weight.T, payload, "fetch_steps", 1)],
        [((rows, wide + 128), f32), ((longs, 2 * rows, 2 * own), bf16)],
        2 * rows * longs * own * (wide + heads + 1024),
    )
    small = total_over(small, "short")
    inverse = lax.rsqrt(small[:, -1:] / WIDTH + epsilon)
    group_raw = small[:, :wide] * inverse
    step_raw = lax.dynamic_slice_in_dim(small, wide + at_short * heads_here, heads_here, 1) * inverse

    mine, other = call(
        functools.partial(gates_body, own, width),
        "gates",
        [at_long, chip, core],
        [spread],
        [((chips, 2, rows, width), f32), ((chips, 2, rows, width), bf16)],
        2 * 128 * gate_in_weight.size,
        gate_in_weight,
        [
            pltpu.VMEM(gate_in_weight.shape, bf16),
            pltpu.VMEM((shorts, 2 * rows, width), f32),
            pltpu.SemaphoreType.DMA((2 * longs,)),
        ],
        46 * MIB,
    )
    mine = mine + swap(other, "short", 1).astype(f32)
    gate_in = mine[0]
    for q in range(1, chips):
        gate_in = gate_in + swap(mine[q].astype(bf16), "short", 2 * q).astype(f32)
    gate_in = gate_in * inverse

    group_window = jnp.concatenate([group_conv_state, group_raw[:, None, :]], axis=1)
    group_act = jax.nn.silu(jnp.sum(group_window * group_conv_weight[None], axis=1))
    low, high = group_act[:, :STATE], group_act[:, STATE:]
    one = lax.ppermute(jnp.where(at_long < 2, high, low), "long", [(0, 1), (1, 3), (2, 0), (3, 2)])
    two = lax.ppermute(jnp.where(at_long == 1, low, high), "long", [(1, 2), (2, 1)])
    state_in = jnp.where(at_long == 0, low, jnp.where(at_long == 2, two, one))
    state_out = jnp.where(at_long == 3, high, jnp.where(at_long == 1, two, one))
    products = state_products(ssm_state, state_out)

    step_size = jax.nn.softplus(step_raw + step_bias[None])
    decay = jnp.exp(-jnp.exp(decay_log)[None] * step_size)
    window = jnp.concatenate([conv_state, gate_in[1][:, None, :]], axis=1)
    mixer_input = jax.nn.silu(jnp.sum(window * conv_weight[None], axis=1))
    inputs = jnp.repeat(step_size, HEAD_DIM, axis=1) * mixer_input
    readout = jnp.repeat(decay, HEAD_DIM, axis=1) * products
    readout = readout + inputs * jnp.sum(state_in * state_out, axis=1, keepdims=True)
    readout = readout + jnp.repeat(skip_scale, HEAD_DIM)[None] * mixer_input
    readout = readout * jax.nn.silu(gate_in[0])

    unscaled = (readout * norm_gain[None]).astype(bf16)
    payload = with_square(unscaled, jnp.sum(readout * readout, axis=1))
    mixed_weight = fetched(out_weight, payload, "fetch_mixed")
    blocks = exchanged(payload, "short")
    mixed = call(
        functools.partial(out_body, own, width, INNER // GROUPS, shorts),
        "mixed",
        [at_short, at_long],
        [*blocks, mixed_weight],
        [((rows, own), f32)] + [((rows, own), bf16)] * (longs - 1),
        2 * rows * out_weight.size,
    )
    half_rows = rows // 2
    new_state = updated(ssm_state, decay, inputs, state_in, 0, half_rows, None, mixed[-1], "update_first")
    arrived = [swap(mixed[k], "long", k) for k in range(longs - 1, 0, -1)]
    *arrived, new_state = lax.optimization_barrier((*arrived, new_state))
    total = features + mixed[0]
    for block in arrived:
        total = total + block.astype(f32)
    middle = total.astype(bf16).astype(f32)

    scaled_own = (middle * mlp_gain.astype(f32)).astype(bf16)
    payload = with_square(scaled_own, jnp.sum(middle * middle, axis=1))
    upward_weight = fetched(up_weight, payload, "fetch_upward")
    blocks = exchanged(payload, "long")
    half = up_weight.shape[1] // 2
    mine, other = call(
        functools.partial(up_body, own),
        "upward",
        [at_long, core],
        [*blocks, upward_weight],
        [((rows, half + 128), f32), ((rows, half + 128), bf16)],
        2 * rows * up_weight.size,
    )

    def added(to, arrived):
        square = to[:, half:] + square_of(arrived[:, half:])[:, None]
        return jnp.concatenate([to[:, :half] + arrived[:, :half].astype(f32), square], axis=1)

    upward = added(mine, swap(other, "short", 1))
    sent = with_square(upward[:, :half].astype(bf16), upward[:, half])
    downward_weight = fetched(down_weight, sent, "fetch_downward")
    for k in range(1, chips):
        arrived, downward_weight = lax.optimization_barrier((swap(sent, "short", 2 * k), downward_weight))
        upward = added(upward, arrived)
    inverse_mid = lax.rsqrt(upward[:, half:][:, :1] / WIDTH + epsilon)
    active = jnp.square(jnp.maximum(upward[:, :half] * inverse_mid, 0.0)).astype(bf16)
    parts = call(
        functools.partial(down_body, own),
        "downward",
        [core, at_long],
        [active, swap(active, "short", 1), downward_weight],
        [((rows, own), f32)] + [((rows, own), bf16)] * (longs - 1),
        2 * rows * down_weight.size,
    )
    new_state = updated(ssm_state, decay, inputs, state_in, half_rows, rows - half_rows, new_state, parts[-1], "update_last")
    arrived = [swap(parts[k], "long", k) for k in range(longs - 1, 0, -1)]
    *arrived, new_state = lax.optimization_barrier((*arrived, new_state))
    total = middle + parts[0]
    for block in arrived:
        total = total + block.astype(f32)
    return (total.astype(bf16), new_state, window[:, 1:], group_window[:, 1:])


def solution(mesh):
    whole_groups = mesh.shape["long"] == GROUPS and mesh.shape["short"] == 4
    placed = (
        P("groups", ("short", "long")),
        P(("short", "long")),
        P(("short", "long")),
        P("short", None, "long"),
        P("short", "long"),
        P("short", "long"),
        P(("long", "short")),
        P(("long", "short")),
        P(("long", "short")),
        P(None, ("long", "short")),
        P(None, "long"),
        P("groups", None, ("long", "short")),
        P("groups", None, "long"),
        P("groups", ("long", "short"), None, None),
        P(("long", "short")),
        P("long", "short"),
        P("short", "long"),
        P("long", "short"),
    )
    return jax.shard_map(
        fast if whole_groups else local,
        mesh=mesh,
        in_specs=placed,
        out_specs=(
            P("groups", ("short", "long")),
            P("groups", ("long", "short"), None, None),
            P("groups", None, ("long", "short")),
            P("groups", None, "long"),
        ),
        check_vma=False,
    )
```
